128 devices in a mesh: corpus: 32 (over y, x, core), query: 4 (over z).
Axes of the slice: x: 4, y: 4, z: 4, core: 2. Of those that a mesh axis runs over, the one named last changes fastest.
Arguments:
- corpus_hidden: bfloat16 [1024, 64, 14336], P(('corpus', 'query')), may hold values from -48 to 48
- corpus_grad: bfloat16 [1024, 64, 4096], P(('corpus', 'query')), may hold values from -6 to 6
- corpus_lengths: int32 [1024], P(('corpus', 'query')), may hold values from 16 to 64
- query_hidden: bfloat16 [256, 64, 14336], P(('corpus', 'query')), may hold values from -6 to 6
- query_grad: bfloat16 [256, 64, 4096], P(('corpus', 'query')), may hold values from -6 to 6
- query_lengths: int32 [256], P(('corpus', 'query')), may hold values from 16 to 64
- proj_in: bfloat16 [14336, 64], replicated, may hold values from -0.046875 to 0.046875
- proj_out: bfloat16 [4096, 64], replicated, may hold values from -0.09375 to 0.09375
Outputs:
- scores: float32 [1024, 256], P(('corpus', 'query'))
The draws below stay inside these ranges and needn't reach their ends.
All inputs are finite; a program needn't handle non-finite values.
Results may differ from the reference program's by a relative error of at most 0.0003.
Values sent between devices are 32-bit elements; how exact they have to be, the bound alone decides.
A program may use at most 128 MiB of HBM per device.

```python
import jax
import jax.numpy as jnp
from jax import lax

D = 4096
FF = 14336
RANK = 64
LEN = 64
CEX = 1024
QEX = 256


def draw_corpus_hidden(key, part):
    key = jax.random.fold_in(key, 11)
    first, second = jax.random.split(key, 2)
    rows = (jnp.arange(CEX, dtype=jnp.float32) / CEX)[:, None, None]
    base = jax.random.truncated_normal(first, -6.0, 6.0, (CEX, LEN, FF), jnp.float32)
    scale = 3.0 ** rows * jnp.exp(jax.random.uniform(second, (CEX, 1, 1), jnp.float32, 0.0, 0.7))
    return (base * scale).astype(jnp.bfloat16)


def with_ends(entries, own_key, smallest, largest):
    index_at = [jax.random.randint(jax.random.fold_in(own_key, axis), (), 0, length) for axis, length in enumerate(entries.shape)]
    main_axis = entries.shape.index(max(entries.shape))
    next_to = index_at[:main_axis] + [(index_at[main_axis] + 1) % entries.shape[main_axis]] + index_at[main_axis + 1:]
    return entries.at[tuple(index_at)].set(smallest).at[tuple(next_to)].set(largest)


def level_of(key, extent, cuts, smallest, largest):
    def one(axis_at, parts):
        draws = jax.random.uniform(jax.random.fold_in(jax.random.fold_in(key, 6), axis_at), (parts,), jnp.float32, smallest / len(cuts), largest / len(cuts))
        return jnp.repeat(jnp.exp(draws), extent[axis_at] // parts).reshape((-1,) + (1,) * (len(extent) - axis_at - 1))

    gain = one(*cuts[0])
    for cut in cuts[1:]:
        gain = gain * one(*cut)
    return gain


def centred(key, dims, deviation, reach, cuts=(), kind=jnp.bfloat16):
    entries = deviation * jax.random.normal(key, dims, jnp.float32)
    if cuts:
        entries = entries * level_of(key, dims, cuts, -0.22, 0.18)
    return jnp.clip(entries, -reach, reach).astype(kind)


def setup_inputs(seed: int = 0) -> dict:
    key_list = jax.random.split(jax.random.key(seed), 9)
    corpus_hidden = draw_corpus_hidden(jax.random.fold_in(key_list[8], 71), 0)
    corpus_grad = centred(key_list[1], (CEX, LEN, D), 1.0, 6.0, ((0, 128),))
    corpus_lengths = with_ends(jax.random.randint(key_list[2], (CEX,), LEN // 4, LEN + 1), jax.random.fold_in(key_list[2], 1), LEN // 4, LEN).astype(jnp.int32)
    query_hidden = centred(key_list[3], (QEX, LEN, FF), 1.0, 6.0, ((0, 128),))
    query_grad = centred(key_list[4], (QEX, LEN, D), 1.0, 6.0, ((0, 128),))
    query_lengths = with_ends(jax.random.randint(key_list[5], (QEX,), LEN // 4, LEN + 1), jax.random.fold_in(key_list[5], 1), LEN // 4, LEN).astype(jnp.int32)
    proj_in = centred(key_list[6], (FF, RANK), FF ** -0.5, 0.046875)
    proj_out = centred(key_list[7], (D, RANK), D ** -0.5, 0.09375)
    return dict(corpus_hidden=corpus_hidden, corpus_grad=corpus_grad, corpus_lengths=corpus_lengths, query_hidden=query_hidden, query_grad=query_grad, query_lengths=query_lengths, proj_in=proj_in, proj_out=proj_out)


def project(hidden, grad, lengths, proj_in, proj_out):
    slots = lax.broadcasted_iota(jnp.int32, (1, hidden.shape[1]), 1)
    live = (slots < lengths[:, None]).astype(jnp.float32)[:, :, None]
    in_side = jnp.einsum('etf,fk->etk', hidden.astype(jnp.float32), proj_in.astype(jnp.float32), preferred_element_type=jnp.float32) * live
    out_side = jnp.einsum('etf,fk->etk', grad.astype(jnp.float32), proj_out.astype(jnp.float32), preferred_element_type=jnp.float32) * live
    grads = jnp.einsum('etk,etj->ekj', out_side, in_side, precision=lax.Precision.HIGHEST)
    return (in_side, out_side, grads)

def invert(fisher):
    width = fisher.shape[0]
    eye = jnp.eye(width, dtype=jnp.float32)
    damped = fisher + 0.1 * jnp.trace(fisher) / width * eye
    factor = jnp.linalg.cholesky(damped)
    return jax.scipy.linalg.cho_solve((factor, True), eye)

def reference(corpus_hidden, corpus_grad, corpus_lengths, query_hidden, query_grad, query_lengths, proj_in, proj_out):
    in_corpus, out_corpus, grad_corpus = project(corpus_hidden, corpus_grad, corpus_lengths, proj_in, proj_out)
    unused_in, unused_out, grad_query = project(query_hidden, query_grad, query_lengths, proj_in, proj_out)
    fisher_in = jnp.einsum('etk,etj->kj', in_corpus, in_corpus, precision=lax.Precision.HIGHEST)
    fisher_out = jnp.einsum('etk,etj->kj', out_corpus, out_corpus, precision=lax.Precision.HIGHEST)
    inv_in = invert(fisher_in)
    inv_out = invert(fisher_out)
    left_done = jnp.einsum('ij,njk->nik', inv_out, grad_query, precision=lax.Precision.HIGHEST)
    precond = jnp.einsum('nik,kl->nil', left_done, inv_in, precision=lax.Precision.HIGHEST)
    flat_corpus = grad_corpus.reshape(grad_corpus.shape[0], -1)
    flat_query = precond.reshape(precond.shape[0], -1)
    return jnp.einsum('ek,qk->eq', flat_corpus, flat_query, precision=lax.Precision.HIGHEST)
```

```python
import jax
import jax.numpy as jnp
from jax import lax
from jax.experimental import pallas as pl
from jax.experimental.pallas import tpu as pltpu
from jax.sharding import PartitionSpec as P

F32 = jnp.float32
BF16 = jnp.bfloat16
HIGHEST = lax.Precision.HIGHEST
MESH = pl.DeviceIdType.MESH
BY_ROWS = (((1,), (1,)), ((), ()))
BY_TOKENS = (((0,), (0,)), ((), ()))

RANK = 64
LEN = 64
SIDE = 4
CHIPS = SIDE * SIDE
MEMBERS = 2 * SIDE
DEVICES = CHIPS * MEMBERS

PARTS = ((0, 24, (2, 1, 0)), (24, 24, (1, 0, 2)), (48, 16, (0, 2, 1)))


def coordinates():
    corpus = lax.axis_index("corpus")
    z = lax.axis_index("query")
    return corpus % 2, (corpus // 2) % SIDE, corpus // (2 * SIDE), z


def device(core, y, x, z):
    return ((y * SIDE + x) * 2 + core, z)


def iota(shape, axis):
    return lax.broadcasted_iota(jnp.int32, shape, axis)


def spread(block, row):
    return jnp.broadcast_to(block[row : row + 1], block.shape)


def exact_dot(a, b, dims):
    return lax.dot_general(a, b, dims, precision=HIGHEST, preferred_element_type=F32)


def plain_dot(a, b, dims):
    return lax.dot_general(a, b, dims, preferred_element_type=F32)


def damp(fisher):
    row, lane = iota(fisher.shape, 0), iota(fisher.shape, 1)
    diag_in = row == lane
    diag_out = row + RANK == lane
    trace_in = jnp.sum(jnp.where(diag_in, fisher, 0.0))
    trace_out = jnp.sum(jnp.where(diag_out, fisher, 0.0))
    fisher = fisher + jnp.where(diag_in, 0.1 * trace_in / RANK, 0.0)
    return fisher + jnp.where(diag_out, 0.1 * trace_out / RANK, 0.0)


def invert_pair(pair):
    step = 8
    count = RANK // step
    shape = (step, 2 * RANK)
    rows = [pair[step * i : step * (i + 1)] for i in range(count)]
    lane, row = iota(shape, 1), iota(shape, 0)
    column = lane % RANK
    for b in range(count):
        inside = (column >= step * b) & (column < step * (b + 1))
        picked = [
            [
                jnp.take_along_axis(rows[o], jnp.where(lane < RANK, step * b + j, RANK + step * b + j), axis=1)
                for j in range(step)
            ]
            for o in range(count)
        ]
        d = [[spread(picked[b][j], i) if j >= i else None for j in range(step)] for i in range(step)]
        r = [
            jnp.where(inside, jnp.where(column == step * b + i, 1.0, 0.0), spread(rows[b], i))
            for i in range(step)
        ]
        for k in range(step):
            pivot = 1.0 / d[k][k]
            u = [None] * step
            for j in range(k + 1, step):
                u[j] = d[k][j] * pivot
            for i in range(k + 1, step):
                for j in range(i, step):
                    d[i][j] = d[i][j] - u[i] * d[k][j]
                r[i] = r[i] - u[i] * r[k]
            r[k] = r[k] * pivot
            for j in range(k + 1, step):
                d[k][j] = u[j]
        for k in range(step - 1, 0, -1):
            for i in range(k):
                r[i] = r[i] - d[i][k] * r[k]
        for o in range(count):
            if o == b:
                block = r[0]
                for i in range(1, step):
                    block = jnp.where(row == i, r[i], block)
                rows[o] = block
                continue
            t = [picked[o][j] * r[j] for j in range(step)]
            total = ((t[0] + t[1]) + (t[2] + t[3])) + ((t[4] + t[5]) + (t[6] + t[7]))
            rows[o] = jnp.where(inside, 0.0, rows[o]) - total
    return jnp.concatenate(rows, axis=0)


def split(values):
    high = values.astype(BF16)
    low = (values - high.astype(F32)).astype(BF16)
    return high, low


OUT_CUTS = ((0, 2048), (2048, 2048))
IN_CUTS = ((0, 4096), (4096, 4096), (8192, 4096), (12288, 2048))


def kernel(
    corpus_hidden,
    corpus_grad,
    corpus_lengths,
    query_hidden,
    query_grad,
    query_lengths,
    proj_in,
    proj_out,
    out,
    v_ch,
    v_cg,
    v_qh,
    v_qg,
    v_pin,
    v_pout,
    grads,
    slabs,
    q_high,
    q_low,
    part,
    piece,
    from_members,
    from_plane,
    fisher,
    turned,
    local_sem,
    sum_send,
    sum_recv,
    slab_send,
    slab_recv,
    pair_send,
    pair_recv,
):
    core, x, y, z = coordinates()
    me = (y, x, z)
    member, place = core * SIDE + z, y * SIDE + x
    examples = corpus_hidden.shape[0] // LEN
    queries = query_hidden.shape[0] // LEN

    copies = {}

    def bring(name, src, dst, cut):
        at, width = cut
        copy = pltpu.make_async_copy(
            src.at[:, pl.ds(at, width)], dst.at[:, pl.ds(at, width)], local_sem.at[len(copies)]
        )
        copy.start()
        copies[name, at] = copy

    for cut in OUT_CUTS:
        bring("pout", proj_out, v_pout, cut)
        bring("qg", query_grad, v_qg, cut)
    for cut in IN_CUTS:
        bring("pin", proj_in, v_pin, cut)
        bring("qh", query_hidden, v_qh, cut)
    for cut in OUT_CUTS:
        bring("cg", corpus_grad, v_cg, cut)
    for cut in IN_CUTS:
        bring("ch", corpus_hidden, v_ch, cut)

    barrier = pltpu.get_barrier_semaphore()

    def member_at(d):
        t = (member + d) % MEMBERS
        return device(t // SIDE, y, x, t % SIDE)

    def place_at(d):
        t = (place + d) % CHIPS
        return device(core, t // SIDE, t % SIDE, z)

    for d in range(1, MEMBERS):
        pl.semaphore_signal(barrier, inc=1, device_id=member_at(d), device_id_type=MESH)
    for d in range(1, CHIPS):
        pl.semaphore_signal(barrier, inc=1, device_id=place_at(d), device_id_type=MESH)

    def projected(name, src, weight_name, weight, cuts):
        total = None
        for at, width in cuts:
            if weight_name:
                copies[weight_name, at].wait()
            copies[name, at].wait()
            term = plain_dot(src[:, pl.ds(at, width)], weight[:, pl.ds(at, width)], BY_ROWS)
            total = term if total is None else total + term
        return total

    slot = iota((LEN, RANK), 0)

    def masked(values, lengths, count):
        return [
            jnp.where(slot < lengths[e], values[e * LEN : (e + 1) * LEN], 0.0) for e in range(count)
        ]

    out_query = masked(projected("qg", v_qg, "pout", v_pout, OUT_CUTS), query_lengths, queries)
    in_query = masked(projected("qh", v_qh, "pin", v_pin, IN_CUTS), query_lengths, queries)
    lower = iota((RANK // 2, 2 * RANK), 1) < RANK
    mine = slabs.at[y, x, core, z]
    for q in range(queries):
        turned[pl.ds(0, RANK), :] = exact_dot(
            out_query[q], jnp.concatenate([in_query[q], in_query[q]], axis=1), BY_TOKENS
        )
        even = turned[pl.ds(0, RANK // 2, stride=2), :]
        odd = turned[pl.ds(1, RANK // 2, stride=2), :]
        mine[pl.ds(q * RANK // 2, RANK // 2), :] = jnp.where(lower, even, odd)

    pl.semaphore_wait(barrier, MEMBERS - 1 + CHIPS - 1)

    def neighbour(axis, d):
        there = list(me)
        there[axis] = (there[axis] + d) % SIDE
        return device(core, *there)

    def block(p, phase, at, whose):
        first, count, order = PARTS[p]
        index = [pl.ds(0, SIDE) if k in order[:phase] else me[k] for k in range(3)]
        index[order[phase]] = at
        return slabs.at[index[0], index[1], whose, index[2], pl.ds(first, count)]

    def send_block(p, phase):
        axis = PARTS[p][2][phase]
        ref = block(p, phase, me[axis], core)
        for d in (2, 1, 3):
            pltpu.make_async_remote_copy(
                src_ref=ref,
                dst_ref=ref,
                send_sem=slab_send.at[p, phase],
                recv_sem=slab_recv.at[p, phase],
                device_id=neighbour(axis, d),
                device_id_type=MESH,
            ).start()

    def wait_block(p, phase, sem):
        ref = block(p, phase, pl.ds(0, SIDE - 1), core)
        pltpu.make_async_copy(ref, ref, sem.at[p, phase]).wait()

    def pair_copy(p):
        first, count, _ = PARTS[p]
        ref = slabs.at[:, :, core, :, pl.ds(first, count)]
        return pltpu.make_async_remote_copy(
            src_ref=ref,
            dst_ref=ref,
            send_sem=pair_send.at[p],
            recv_sem=pair_recv.at[p],
            device_id=device(1 - core, y, x, z),
            device_id_type=MESH,
        )

    everyone = range(len(PARTS))
    for p in everyone:
        send_block(p, 0)

    outs = masked(projected("cg", v_cg, None, v_pout, OUT_CUTS), corpus_lengths, examples)
    ins = projected("ch", v_ch, None, v_pin, IN_CUTS[:2])
    for p in everyone:
        wait_block(p, 0, slab_recv)
        send_block(p, 1)
    ins = ins + projected("ch", v_ch, None, v_pin, IN_CUTS[2:])
    ins = masked(ins, corpus_lengths, examples)
    both = jnp.concatenate(
        [jnp.concatenate([i, o], axis=1) for i, o in zip(ins, outs)], axis=0
    )
    gram = exact_dot(both, both, BY_TOKENS)
    lower = iota((RANK, 2 * RANK), 1) < RANK
    part[...] = jnp.where(lower, gram[:RANK], gram[RANK:])

    def octet(t):
        return pl.ds(pl.multiple_of(t * 8, 8), 8)

    def send_sum(stage, src, dst, to):
        pltpu.make_async_remote_copy(
            src_ref=src,
            dst_ref=dst,
            send_sem=sum_send.at[stage],
            recv_sem=sum_recv.at[stage],
            device_id=to,
            device_id_type=MESH,
        ).start()

    def wait_all(ref, sem):
        pltpu.make_async_copy(ref, ref, sem).wait()

    for d in range(1, MEMBERS):
        send_sum(0, part.at[octet((member + d) % MEMBERS)], from_members.at[d - 1], member_at(d))
    for e in range(examples):
        grads[pl.ds(e * RANK, RANK), :] = exact_dot(outs[e], ins[e], BY_TOKENS)
    for p in everyone:
        wait_block(p, 1, slab_recv)
        send_block(p, 2)
    wait_all(from_members, sum_recv.at[0])
    total = part[octet(member), :]
    for d in range(MEMBERS - 1):
        total = total + from_members[d]
    piece[...] = total
    for d in range(1, CHIPS):
        send_sum(1, piece, from_plane.at[d - 1], place_at(d))
    wait_all(from_plane, sum_recv.at[1])
    for d in range(CHIPS - 1):
        total = total + from_plane[d]
    fisher[octet(member), :] = total
    for d in range(1, MEMBERS):
        send_sum(2, fisher.at[octet(member)], fisher.at[octet(member)], member_at(d))
    for p in everyone:
        wait_block(p, 2, slab_recv)
        pair_copy(p).start()
    wait_all(from_members, sum_recv.at[2])

    inverse = invert_pair(damp(fisher[...]))
    swapped = pltpu.roll(inverse, RANK, 1)
    twice_in = jnp.where(lower, inverse, swapped)
    right_done = exact_dot(grads[...], twice_in, (((1,), (0,)), ((), ())))
    right_done = jnp.concatenate(
        [right_done[e * RANK : (e + 1) * RANK] for e in range(examples)], axis=1
    )
    done = exact_dot(swapped[:, :RANK], right_done, (((1,), (0,)), ((), ())))
    for e in range(examples):
        turned[pl.ds(e * RANK, RANK), :] = done[:, e * 2 * RANK : (e + 1) * 2 * RANK]
    lower = iota((examples, 2 * RANK), 1) < RANK
    left = jnp.concatenate(
        [
            jnp.where(
                lower,
                turned[pl.ds(i, examples, stride=RANK), :],
                turned[pl.ds(i + 1, examples, stride=RANK), :],
            )
            for i in range(0, RANK, 2)
        ],
        axis=1,
    )
    left_high = left.astype(BF16).astype(F32)
    left_both = jnp.concatenate([left_high, left - left_high], axis=0).astype(BF16)

    for p in everyone:
        pair_copy(p).wait_recv()
    flat = slabs.reshape(DEVICES * RANK, 2 * RANK)
    half = RANK // 2
    for q in range(queries):
        for i in range(half):
            high, low = split(flat[pl.ds(q * half + i, DEVICES, stride=RANK), :])
            q_high[pl.ds(q * DEVICES, DEVICES), pl.ds(i * 2 * RANK, 2 * RANK)] = high
            q_low[pl.ds(q * DEVICES, DEVICES), pl.ds(i * 2 * RANK, 2 * RANK)] = low
    main = plain_dot(q_high[...], left_both, BY_ROWS)
    rest = plain_dot(q_low[...], left_both, BY_ROWS)
    main = main.T
    rest = rest.T
    scores = main[:examples] + main[examples:] + rest[:examples]
    out[...] = scores

    for p in everyone:
        for phase in range(3):
            wait_block(p, phase, slab_send)
        pair_copy(p).wait_send()
    wait_all(from_members, sum_send.at[0])
    wait_all(from_plane, sum_send.at[1])
    wait_all(from_members, sum_send.at[2])


def per_device(
    corpus_hidden,
    corpus_grad,
    corpus_lengths,
    query_hidden,
    query_grad,
    query_lengths,
    proj_in,
    proj_out,
):
    examples = corpus_hidden.shape[0]
    queries = query_hidden.shape[0]
    flat = lambda a: a.reshape(-1, a.shape[-1])
    anywhere = pl.BlockSpec(memory_space=pl.ANY)
    scalars = pl.BlockSpec(memory_space=pltpu.SMEM)
    operands = (
        flat(corpus_hidden),
        flat(corpus_grad),
        corpus_lengths,
        flat(query_hidden),
        flat(query_grad),
        query_lengths,
        proj_in.T,
        proj_out.T,
    )
    big = [operands[k] for k in (0, 1, 3, 4, 6, 7)]
    dma = pltpu.SemaphoreType.DMA
    scores = pl.pallas_call(
        kernel,
        out_shape=jax.ShapeDtypeStruct((examples, queries * DEVICES), F32),
        in_specs=[anywhere, anywhere, scalars, anywhere, anywhere, scalars, anywhere, anywhere],
        out_specs=pl.BlockSpec(memory_space=pltpu.VMEM),
        scratch_shapes=[pltpu.VMEM(a.shape, BF16) for a in big]
        + [
            pltpu.VMEM((examples * RANK, RANK), F32),
            pltpu.VMEM((SIDE, SIDE, 2, SIDE, RANK, 2 * RANK), F32),
            pltpu.VMEM((queries * DEVICES, RANK * RANK), BF16),
            pltpu.VMEM((queries * DEVICES, RANK * RANK), BF16),
            pltpu.VMEM((RANK, 2 * RANK), F32),
            pltpu.VMEM((8, 2 * RANK), F32),
            pltpu.VMEM((MEMBERS - 1, 8, 2 * RANK), F32),
            pltpu.VMEM((CHIPS - 1, 8, 2 * RANK), F32),
            pltpu.VMEM((RANK, 2 * RANK), F32),
            pltpu.VMEM((examples * RANK, 2 * RANK), F32),
            dma((24,)),
            dma((3,)),
            dma((3,)),
            dma((3, 3)),
            dma((3, 3)),
            dma((3,)),
            dma((3,)),
        ],
        compiler_params=pltpu.CompilerParams(
            collective_id=0, has_side_effects=True, vmem_limit_bytes=60 * 1024 * 1024
        ),
        name="influence",
    )(*operands)
    return scores.reshape(examples, queries, DEVICES).transpose(0, 2, 1).reshape(examples, -1)


def solution(mesh):
    placed = (
        P(("corpus", "query"), None, None),
        P(("corpus", "query"), None, None),
        P(("corpus", "query")),
        P(("corpus", "query"), None, None),
        P(("corpus", "query"), None, None),
        P(("corpus", "query")),
        P(),
        P(),
    )
    return jax.shard_map(
        per_device,
        mesh=mesh,
        in_specs=placed,
        out_specs=P(("corpus", "query"), None),
        check_vma=False,
    )
```

```python
import jax
import jax.numpy as jnp
from jax import lax
from jax.experimental import pallas as pl
from jax.experimental.pallas import tpu as pltpu
from jax.sharding import PartitionSpec as P

F32 = jnp.float32
BF16 = jnp.bfloat16
MESH = pl.DeviceIdType.MESH
BY_ROWS = (((1,), (1,)), ((), ()))
BY_COLUMNS = (((1,), (0,)), ((), ()))

RANK = 64
LEN = 64
SIDE = 4
CHIPS = SIDE * SIDE
MEMBERS = 2 * SIDE
DEVICES = CHIPS * MEMBERS

PARTS = ((0, 24, (2, 1, 0)), (24, 24, (1, 0, 2)), (48, 16, (0, 2, 1)))
EVERYONE = range(len(PARTS))
STEPS = (1, 3, 2)


def coordinates():
    corpus = lax.axis_index("corpus")
    z = lax.axis_index("query")
    return corpus % 2, (corpus // 2) % SIDE, corpus // (2 * SIDE), z


def device(core, y, x, z):
    return ((y * SIDE + x) * 2 + core, z)


def iota(shape, axis):
    return lax.broadcasted_iota(jnp.int32, shape, axis)


def spread(block, row):
    return jnp.broadcast_to(block[row : row + 1], block.shape)


def plain_dot(a, b, dims):
    return lax.dot_general(a, b, dims, preferred_element_type=F32)


def damp(fisher):
    row, lane = iota(fisher.shape, 0), iota(fisher.shape, 1)
    diag = row == lane % RANK
    held = jnp.sum(jnp.where(diag, fisher, 0.0), axis=0, keepdims=True)
    lower = iota(held.shape, 1) < RANK
    trace_in = jnp.sum(jnp.where(lower, held, 0.0), axis=1, keepdims=True)
    trace_out = jnp.sum(jnp.where(lower, 0.0, held), axis=1, keepdims=True)
    shift = 0.1 / RANK * jnp.where(lower, trace_in, trace_out)
    return fisher + jnp.where(diag, shift, 0.0)


def invert_pair(pair):
    step = 8
    count = RANK // step
    shape = (step, 2 * RANK)
    lane, row = iota(shape, 1), iota(shape, 0)
    column = lane % RANK

    def eliminate(b, carry):
        first = pl.multiple_of(b * step, step)
        panel_at = pl.ds(first, step)
        offset = column - first
        inside = (offset >= 0) & (offset < step)
        where_j = [jnp.where(lane < RANK, 0, RANK) + first + j for j in range(step)]
        pick = lambda block: [jnp.take_along_axis(block, at, axis=1) for at in where_j]
        panel = pair[panel_at, :]
        picked = pick(panel)
        d = [[spread(picked[j], i) if j >= i else None for j in range(step)] for i in range(step)]
        r = [jnp.where(inside, jnp.where(offset == i, 1.0, 0.0), spread(panel, i)) for i in range(step)]
        for k in range(step):
            pivot = 1.0 / d[k][k]
            u = [None] * step
            for j in range(k + 1, step):
                u[j] = d[k][j] * pivot
            for i in range(k + 1, step):
                for j in range(i, step):
                    d[i][j] = d[i][j] - u[i] * d[k][j]
                r[i] = r[i] - u[i] * r[k]
            r[k] = r[k] * pivot
            for j in range(k + 1, step):
                d[k][j] = u[j]
        for k in range(step - 1, 0, -1):
            for i in range(k):
                r[i] = r[i] - d[i][k] * r[k]
        for o in range(count):
            at = pl.ds(o * step, step)
            block = pair[at, :]
            t = [c * rj for c, rj in zip(pick(block), r)]
            total = ((t[0] + t[1]) + (t[2] + t[3])) + ((t[4] + t[5]) + (t[6] + t[7]))
            pair[at, :] = jnp.where(inside, 0.0, block) - total
        block = r[0]
        for i in range(1, step):
            block = jnp.where(row == i, r[i], block)
        pair[panel_at, :] = block
        return carry

    lax.fori_loop(0, count, eliminate, 0)


def split(values):
    high = values.astype(BF16)
    low = (values - high.astype(F32)).astype(BF16)
    return high, low


def left_of(values, axis):
    high, low = split(values)
    return jnp.concatenate([high, low, high], axis=axis)


def right_of(values, axis):
    high, low = split(values)
    return jnp.concatenate([high, high, low], axis=axis)


def gradients(out_side, in_side):
    lower = iota(out_side.shape, 1) < LEN
    left = jnp.concatenate(
        [left_of(jnp.where(lower, out_side, 0.0), 1), left_of(jnp.where(lower, 0.0, out_side), 1)], axis=0
    )
    right = right_of(in_side, 1)
    return plain_dot(left, jnp.concatenate([right, right], axis=0), BY_ROWS)


OUT_CUTS = ((0, 4096, 1),)
QUERY_CUTS = ((0, 3584, 4),)
CORPUS_CUTS = ((0, 4096, 1), (4096, 4096, 2), (12288, 2048, 1))


def kernel(
    corpus_hidden,
    corpus_grad,
    corpus_lengths,
    query_hidden,
    query_grad,
    query_lengths,
    proj_in,
    proj_out,
    out,
    v_ch,
    v_cg,
    v_qh,
    v_qg,
    v_pin,
    v_pout,
    in_corpus,
    out_corpus,
    in_query,
    out_query,
    grads,
    slabs,
    q_high,
    q_low,
    part,
    piece,
    from_members,
    from_plane,
    fisher,
    turned,
    ahead,
    query_sem,
    corpus_sem,
    weight_sem,
    sum_send,
    sum_recv,
    slab_send,
    slab_recv,
    pair_send,
    pair_recv,
):
    core, x, y, z = coordinates()
    me = (y, x, z)
    member, place = core * SIDE + z, y * SIDE + x
    examples = corpus_hidden.shape[0] // LEN
    queries = query_hidden.shape[0] // LEN

    def bring(one, cut, k):
        src, dst, sem, first = one
        begin, width, _ = cut
        at = pl.ds(pl.multiple_of(begin + k * width, width), width)
        return pltpu.make_async_copy(src.at[:, at], dst.at[:, at], sem.at[first + begin // 1024 + k])

    def bring_all(cuts, *what):
        for cut in cuts:

            def start(k, carry):
                for one in what:
                    bring(one, cut, k).start()
                return carry

            lax.fori_loop(0, cut[2], start, 0)

    last = proj_in.shape[1] // 1024
    pout = (proj_out, v_pout, weight_sem, last)
    pin = (proj_in, v_pin, weight_sem, 0)
    qg = (query_grad, v_qg, query_sem, last)
    qh = (query_hidden, v_qh, query_sem, 0)
    cg = (corpus_grad, v_cg, corpus_sem, last)
    ch = (corpus_hidden, v_ch, corpus_sem, 0)
    bring_all(OUT_CUTS, pout, qg)
    bring_all(QUERY_CUTS, pin, qh)
    bring_all(OUT_CUTS, cg)
    bring_all(CORPUS_CUTS, ch)

    barrier = pltpu.get_barrier_semaphore()

    def member_at(d):
        t = (member + d) % MEMBERS
        return device(t // SIDE, y, x, t % SIDE)

    def place_at(d):
        t = (place + d) % CHIPS
        return device(core, t // SIDE, t % SIDE, z)

    for d in range(1, MEMBERS):
        pl.semaphore_signal(barrier, inc=1, device_id=member_at(d), device_id_type=MESH)
    for d in range(1, CHIPS):
        pl.semaphore_signal(barrier, inc=1, device_id=place_at(d), device_id_type=MESH)

    def project(what, weight, total, cuts, also=None):
        for cut in cuts:
            begin, width, count = cut

            def step(k, carry):
                for one in (what, also) if also else (what,):
                    bring(one, cut, k).wait()
                at = pl.ds(pl.multiple_of(begin + k * width, width), width)
                total[...] += plain_dot(what[1][:, at], weight[:, at], BY_ROWS)
                return carry

            lax.fori_loop(0, count, step, 0)

    def clear(total):
        total[...] = jnp.zeros_like(total)

    def sides(in_total, out_total, lengths, count):
        slot = iota((LEN, 2 * RANK), 0)
        both = jnp.concatenate([in_total[...], out_total[...]], axis=1)
        both = [
            jnp.where(slot < lengths[e], both[e * LEN : (e + 1) * LEN], 0.0) for e in range(count)
        ]
        return jnp.concatenate(both, axis=0).T

    for total in (out_query, in_query, out_corpus, in_corpus):
        clear(total)
    project(qg, v_pout, out_query, OUT_CUTS, pout)
    project(qh, v_pin, in_query, QUERY_CUTS, pin)
    both = sides(in_query, out_query, query_lengths, queries)
    half = RANK // 2
    lower = iota((half, 2 * RANK), 1) < RANK
    mine = slabs.at[core, y, x, z]
    turned[pl.ds(0, queries * RANK), :] = gradients(both[RANK:], both[:RANK])
    for q in range(queries):
        even = turned[pl.ds(q * RANK, half, stride=2), :]
        odd = turned[pl.ds(q * RANK + 1, half, stride=2), :]
        mine[pl.ds(q * half, half), :] = jnp.where(lower, even, odd)

    pl.semaphore_wait(barrier, MEMBERS - 1 + CHIPS - 1)

    def block(p, places, whose=core):
        first, count, order = PARTS[p]
        index = [None] * 3
        for axis, place in zip(order, places):
            index[axis] = place
        return slabs.at[whose, index[0], index[1], index[2], pl.ds(first, count)]

    def own(p, phase, d=0):
        return (me[PARTS[p][2][phase]] + SIDE - d) % SIDE

    def to_axis(p, phase, ref, d, sem):
        there = list(me)
        axis = PARTS[p][2][phase]
        there[axis] = (there[axis] + d) % SIDE
        pltpu.make_async_remote_copy(
            src_ref=ref,
            dst_ref=ref,
            send_sem=slab_send.at[p, sem],
            recv_sem=slab_recv.at[p, sem],
            device_id=device(core, *there),
            device_id_type=MESH,
        ).start()

    def to_sibling(p, ref):
        pltpu.make_async_remote_copy(
            src_ref=ref,
            dst_ref=ref,
            send_sem=pair_send.at[p],
            recv_sem=pair_recv.at[p],
            device_id=device(1 - core, y, x, z),
            device_id_type=MESH,
        ).start()

    def wait_all(ref, sem):
        pltpu.make_async_copy(ref, ref, sem).wait()

    every = pl.ds(0, SIDE)
    others = pl.ds(0, SIDE - 1)

    def first_phase():
        for p in EVERYONE:
            ref = block(p, (own(p, 0), own(p, 1), own(p, 2)))
            for d in STEPS:
                to_axis(p, 0, ref, d, 0)

    def second_phase():
        for p in EVERYONE:
            wait_all(block(p, (others, 0, 0)), slab_recv.at[p, 0])
            ref = block(p, (every, own(p, 1), own(p, 2)))
            for d in STEPS:
                to_axis(p, 1, ref, d, d)
            for d in STEPS:
                to_axis(p, 2, ref, d, 3 + d)
            to_sibling(p, ref)

    def third_phase(d):
        for p in EVERYONE:
            ref = block(p, (every, own(p, 1, d), own(p, 2)))
            wait_all(ref, slab_recv.at[p, d])
            for far in STEPS:
                to_axis(p, 2, ref, far, 3 + far)
            to_sibling(p, ref)

    def last_phase(d):
        for p in EVERYONE:
            ref = block(p, (every, every, own(p, 2, d)))
            wait_all(ref, slab_recv.at[p, 3 + d])
            to_sibling(p, ref)

    first_phase()

    project(cg, v_pout, out_corpus, OUT_CUTS)
    project(ch, v_pin, in_corpus, CORPUS_CUTS[:1])
    second_phase()
    project(ch, v_pin, in_corpus, CORPUS_CUTS[1:])
    both = sides(in_corpus, out_corpus, corpus_lengths, examples)
    gram = plain_dot(left_of(both, 1), right_of(both, 1), BY_ROWS)
    lower = iota((RANK, 2 * RANK), 1) < RANK
    part[...] = jnp.where(lower, gram[:RANK], gram[RANK:])

    def octet(t):
        return pl.ds(pl.multiple_of(t * 8, 8), 8)

    def send_sum(stage, src, dst, to):
        pltpu.make_async_remote_copy(
            src_ref=src,
            dst_ref=dst,
            send_sem=sum_send.at[stage],
            recv_sem=sum_recv.at[stage],
            device_id=to,
            device_id_type=MESH,
        ).start()

    for d in range(1, MEMBERS):
        send_sum(0, part.at[octet((member + d) % MEMBERS)], from_members.at[d - 1], member_at(d))
    for d in STEPS:
        third_phase(d)
    for e in range(0, examples, 2):
        tokens = slice(e * LEN, (e + 2) * LEN)
        grads[pl.ds(e * RANK, 2 * RANK), :] = gradients(both[RANK:, tokens], both[:RANK, tokens])
    wait_all(from_members, sum_recv.at[0])
    total = part[octet(member), :]
    for d in range(MEMBERS - 1):
        total = total + from_members[d]
    piece[...] = total
    for d in range(1, CHIPS):
        send_sum(1, piece, from_plane.at[d - 1], place_at(d))
    last_phase(1)
    wait_all(from_plane, sum_recv.at[1])
    for d in range(CHIPS - 1):
        total = total + from_plane[d]
    fisher[octet(member), :] = total
    for d in range(1, MEMBERS):
        send_sum(2, fisher.at[octet(member)], fisher.at[octet(member)], member_at(d))

    for d in STEPS[1:]:
        last_phase(d)
    flat = slabs.reshape(DEVICES * RANK, 2 * RANK)

    def halve(row):
        q, i = row // half, row % half
        high, low = split(flat[pl.ds(row, DEVICES, stride=RANK), :].T)
        at = (
            pl.ds(pl.multiple_of(i * 2 * RANK, 2 * RANK), 2 * RANK),
            pl.ds(pl.multiple_of(q * DEVICES, DEVICES), DEVICES),
        )
        q_high[at] = high
        q_low[at] = low

    def halve_some(b):
        for k in range(8):
            halve(b * 8 + k)

    for p in EVERYONE:
        wait_all(block(p, (every, every, every), 0), pair_recv.at[p])
    lax.fori_loop(0, RANK // 8, lambda b, carry: (halve_some(b), carry)[1], 0)

    wait_all(from_members, sum_recv.at[2])
    pair = turned.at[pl.ds(0, RANK)]
    pair[...] = damp(fisher[...])
    invert_pair(pair)
    inverse = pair[...]
    swapped = pltpu.roll(inverse, RANK, 1)
    twice_in = right_of(jnp.where(lower, inverse, swapped), 0)
    lower = iota((examples * RANK, 2 * RANK), 1) < RANK
    held = grads[...]
    high = held.astype(BF16).astype(F32)
    thrice = jnp.concatenate([jnp.where(lower, high, held - high), high[:, :RANK]], axis=1)
    right_done = plain_dot(thrice.astype(BF16), twice_in, BY_COLUMNS)
    right_done = jnp.concatenate(
        [right_done[e * RANK : (e + 1) * RANK] for e in range(examples)], axis=1
    )
    lower = iota((RANK, 2 * RANK), 1) < RANK
    high = inverse.astype(BF16).astype(F32)
    swapped_high = pltpu.roll(high, RANK, 1)
    thrice = jnp.concatenate([jnp.where(lower, swapped_high, inverse - high), swapped_high[:, :RANK]], axis=1)
    done = plain_dot(thrice.astype(BF16), right_of(right_done, 0), BY_COLUMNS)
    for e in range(examples):
        turned[pl.ds(e * RANK, RANK), :] = done[:, e * 2 * RANK : (e + 1) * 2 * RANK]
    lower = iota((examples, 2 * RANK), 1) < RANK
    left = jnp.concatenate(
        [
            jnp.where(
                lower,
                turned[pl.ds(i, examples, stride=RANK), :],
                turned[pl.ds(i + 1, examples, stride=RANK), :],
            )
            for i in range(0, RANK, 2)
        ],
        axis=1,
    )
    high = left.astype(BF16).astype(F32)
    ahead[...] = jnp.concatenate([high, left - high], axis=0).astype(BF16)

    depth = 512

    def score(k, carry):
        main, rest = carry
        at = pl.ds(pl.multiple_of(k * depth, depth), depth)
        left = ahead[:, at]
        return (
            main + plain_dot(left, q_high[at, :], BY_COLUMNS),
            rest + plain_dot(left, q_low[at, :], BY_COLUMNS),
        )

    none = jnp.zeros((2 * examples, queries * DEVICES), F32)
    main, rest = lax.fori_loop(0, RANK * RANK // depth, score, (none, none))
    scores = main[:examples] + main[examples:] + rest[:examples]
    lane = iota((examples, DEVICES), 1)
    for h in range(queries):
        number = h * DEVICES // queries + lane // queries
        held_at = (number // SIDE) % 2 * (DEVICES // 2) + number // MEMBERS * SIDE + number % SIDE
        picked = [
            jnp.take_along_axis(scores[:, q * DEVICES : (q + 1) * DEVICES], held_at, axis=1)
            for q in range(queries)
        ]
        out[:, pl.ds(h * DEVICES, DEVICES)] = jnp.where(lane % queries == 0, picked[0], picked[1])

    for p in EVERYONE:
        wait_all(block(p, (others, 0, 0)), slab_send.at[p, 0])
        for d in STEPS:
            wait_all(block(p, (every, 0, 0)), slab_send.at[p, d])
            wait_all(block(p, (every, every, 0)), slab_send.at[p, 3 + d])
        wait_all(block(p, (every, every, every), 0), pair_send.at[p])
    wait_all(from_members, sum_send.at[0])
    wait_all(from_plane, sum_send.at[1])
    wait_all(from_members, sum_send.at[2])


def per_device(
    corpus_hidden,
    corpus_grad,
    corpus_lengths,
    query_hidden,
    query_grad,
    query_lengths,
    proj_in,
    proj_out,
):
    examples = corpus_hidden.shape[0]
    queries = query_hidden.shape[0]
    flat = lambda a: a.reshape(-1, a.shape[-1])
    anywhere = pl.BlockSpec(memory_space=pl.ANY)
    scalars = pl.BlockSpec(memory_space=pltpu.SMEM)
    operands = (
        flat(corpus_hidden),
        flat(corpus_grad),
        corpus_lengths,
        flat(query_hidden),
        flat(query_grad),
        query_lengths,
        proj_in.T,
        proj_out.T,
    )
    big = [operands[k] for k in (0, 1, 3, 4, 6, 7)]
    dma = pltpu.SemaphoreType.DMA
    steps = (proj_in.shape[0] + proj_out.shape[0]) // 1024
    scores = pl.pallas_call(
        kernel,
        out_shape=jax.ShapeDtypeStruct((examples, queries * DEVICES), F32),
        in_specs=[anywhere, anywhere, scalars, anywhere, anywhere, scalars, anywhere, anywhere],
        out_specs=pl.BlockSpec(memory_space=pltpu.VMEM),
        scratch_shapes=[pltpu.VMEM(a.shape, BF16) for a in big]
        + [
            pltpu.VMEM((examples * LEN, RANK), F32),
            pltpu.VMEM((examples * LEN, RANK), F32),
            pltpu.VMEM((queries * LEN, RANK), F32),
            pltpu.VMEM((queries * LEN, RANK), F32),
            pltpu.VMEM((examples * RANK, 2 * RANK), F32),
            pltpu.VMEM((2, SIDE, SIDE, SIDE, RANK, 2 * RANK), F32),
            pltpu.VMEM((RANK * RANK, queries * DEVICES), BF16),
            pltpu.VMEM((RANK * RANK, queries * DEVICES), BF16),
            pltpu.VMEM((RANK, 2 * RANK), F32),
            pltpu.VMEM((8, 2 * RANK), F32),
            pltpu.VMEM((MEMBERS - 1, 8, 2 * RANK), F32),
            pltpu.VMEM((CHIPS - 1, 8, 2 * RANK), F32),
            pltpu.VMEM((RANK, 2 * RANK), F32),
            pltpu.VMEM((examples * RANK, 2 * RANK), F32),
            pltpu.VMEM((2 * examples, RANK * RANK), BF16),
            dma((steps,)),
            dma((steps,)),
            dma((steps,)),
            dma((3,)),
            dma((3,)),
            dma((3, 7)),
            dma((3, 7)),
            dma((3,)),
            dma((3,)),
        ],
        compiler_params=pltpu.CompilerParams(
            collective_id=0, has_side_effects=True, vmem_limit_bytes=60 * 1024 * 1024
        ),
        name="influence",
    )(*operands)
    return scores


def solution(mesh):
    placed = (
        P(("corpus", "query"), None, None),
        P(("corpus", "query"), None, None),
        P(("corpus", "query")),
        P(("corpus", "query"), None, None),
        P(("corpus", "query"), None, None),
        P(("corpus", "query")),
        P(),
        P(),
    )
    return jax.shard_map(
        per_device,
        mesh=mesh,
        in_specs=placed,
        out_specs=P(("corpus", "query"), None),
        check_vma=False,
    )
```

```python
import jax
import jax.numpy as jnp
from jax import lax
from jax.experimental import pallas as pl
from jax.experimental.pallas import tpu as pltpu
from jax.sharding import PartitionSpec as P

F32 = jnp.float32
BF16 = jnp.bfloat16
MESH = pl.DeviceIdType.MESH
BY_ROWS = (((1,), (1,)), ((), ()))
BY_COLUMNS = (((1,), (0,)), ((), ()))

RANK = 64
LEN = 64
SIDE = 4
CHIPS = SIDE * SIDE
MEMBERS = 2 * SIDE
DEVICES = CHIPS * MEMBERS
SLAB = 72

PARTS = ((0, 24, (2, 1, 0)), (24, 24, (1, 0, 2)), (48, 16, (0, 2, 1)))
EVERYONE = range(len(PARTS))
STEPS = (1, 3, 2)


def coordinates():
    corpus = lax.axis_index("corpus")
    z = lax.axis_index("query")
    return corpus % 2, (corpus // 2) % SIDE, corpus // (2 * SIDE), z


def device(core, y, x, z):
    return ((y * SIDE + x) * 2 + core, z)


def iota(shape, axis):
    return lax.broadcasted_iota(jnp.int32, shape, axis)


def spread(block, row):
    return jnp.broadcast_to(block[row : row + 1], block.shape)


def plain_dot(a, b, dims):
    return lax.dot_general(a, b, dims, preferred_element_type=F32)


def damp(fisher):
    row, lane = iota(fisher.shape, 0), iota(fisher.shape, 1)
    diag = row == lane % RANK
    held = jnp.sum(jnp.where(diag, fisher, 0.0), axis=0, keepdims=True)
    lower = iota(held.shape, 1) < RANK
    trace_in = jnp.sum(jnp.where(lower, held, 0.0), axis=1, keepdims=True)
    trace_out = jnp.sum(jnp.where(lower, 0.0, held), axis=1, keepdims=True)
    shift = 0.1 / RANK * jnp.where(lower, trace_in, trace_out)
    return fisher + jnp.where(diag, shift, 0.0)


def invert_pair(pair):
    step = 8
    count = RANK // step
    shape = (step, 2 * RANK)
    lane, row = iota(shape, 1), iota(shape, 0)
    column = lane % RANK

    def eliminate(b, carry):
        first = pl.multiple_of(b * step, step)
        panel_at = pl.ds(first, step)
        offset = column - first
        inside = (offset >= 0) & (offset < step)
        where_j = [jnp.where(lane < RANK, 0, RANK) + first + j for j in range(step)]
        pick = lambda block: [jnp.take_along_axis(block, at, axis=1) for at in where_j]
        panel = pair[panel_at, :]
        picked = pick(panel)
        d = [[spread(picked[j], i) if j >= i else None for j in range(step)] for i in range(step)]
        r = [jnp.where(inside, jnp.where(offset == i, 1.0, 0.0), spread(panel, i)) for i in range(step)]
        for k in range(step):
            pivot = 1.0 / d[k][k]
            u = [None] * step
            for j in range(k + 1, step):
                u[j] = d[k][j] * pivot
            for i in range(k + 1, step):
                for j in range(i, step):
                    d[i][j] = d[i][j] - u[i] * d[k][j]
                r[i] = r[i] - u[i] * r[k]
            r[k] = r[k] * pivot
            for j in range(k + 1, step):
                d[k][j] = u[j]
        for k in range(step - 1, 0, -1):
            for i in range(k):
                r[i] = r[i] - d[i][k] * r[k]
        for o in range(count):
            at = pl.ds(o * step, step)
            block = pair[at, :]
            t = [c * rj for c, rj in zip(pick(block), r)]
            total = ((t[0] + t[1]) + (t[2] + t[3])) + ((t[4] + t[5]) + (t[6] + t[7]))
            pair[at, :] = jnp.where(inside, 0.0, block) - total
        block = r[0]
        for i in range(1, step):
            block = jnp.where(row == i, r[i], block)
        pair[panel_at, :] = block
        return carry

    lax.fori_loop(0, count, eliminate, 0)


def split(values):
    high = values.astype(BF16)
    low = (values - high.astype(F32)).astype(BF16)
    return high, low


def left_of(values, axis):
    high, low = split(values)
    return jnp.concatenate([high, low, high], axis=axis)


def right_of(values, axis):
    high, low = split(values)
    return jnp.concatenate([high, high, low], axis=axis)


def gradients(out_side, in_side):
    lower = iota(out_side.shape, 1) < LEN
    left = jnp.concatenate(
        [left_of(jnp.where(lower, out_side, 0.0), 1), left_of(jnp.where(lower, 0.0, out_side), 1)], axis=0
    )
    right = right_of(in_side, 1)
    return plain_dot(left, jnp.concatenate([right, right], axis=0), BY_ROWS)


OUT_CUTS = ((0, 4096, 1),)
QUERY_CUTS = ((0, 3584, 4),)
CORPUS_CUTS = ((0, 4096, 1), (4096, 4096, 2), (12288, 2048, 1))


def kernel(
    corpus_hidden,
    corpus_grad,
    corpus_lengths,
    query_hidden,
    query_grad,
    query_lengths,
    proj_in,
    proj_out,
    out,
    v_ch,
    v_cg,
    v_qh,
    v_qg,
    v_pin,
    v_pout,
    in_corpus,
    out_corpus,
    in_query,
    out_query,
    grads,
    slabs,
    q_high,
    q_low,
    part,
    piece,
    from_members,
    from_plane,
    fisher,
    turned,
    ahead,
    query_sem,
    corpus_sem,
    weight_sem,
    sum_send,
    sum_recv,
    slab_send,
    slab_recv,
    pair_send,
    pair_recv,
):
    core, x, y, z = coordinates()
    me = (y, x, z)
    member, place = core * SIDE + z, y * SIDE + x
    examples = corpus_hidden.shape[0] // LEN
    queries = query_hidden.shape[0] // LEN

    def bring(one, cut, k):
        src, dst, sem, first = one
        begin, width, _ = cut
        at = pl.ds(pl.multiple_of(begin + k * width, width), width)
        return pltpu.make_async_copy(src.at[:, at], dst.at[:, at], sem.at[first + begin // 1024 + k])

    def bring_all(cuts, *what):
        for cut in cuts:

            def start(k, carry):
                for one in what:
                    bring(one, cut, k).start()
                return carry

            lax.fori_loop(0, cut[2], start, 0)

    last = proj_in.shape[1] // 1024
    pout = (proj_out, v_pout, weight_sem, last)
    pin = (proj_in, v_pin, weight_sem, 0)
    qg = (query_grad, v_qg, query_sem, last)
    qh = (query_hidden, v_qh, query_sem, 0)
    cg = (corpus_grad, v_cg, corpus_sem, last)
    ch = (corpus_hidden, v_ch, corpus_sem, 0)
    bring_all(OUT_CUTS, pout, qg)
    bring_all(QUERY_CUTS, pin, qh)
    bring_all(OUT_CUTS, cg)
    bring_all(CORPUS_CUTS, ch)

    barrier = pltpu.get_barrier_semaphore()

    def member_at(d):
        t = (member + d) % MEMBERS
        return device(t // SIDE, y, x, t % SIDE)

    def place_at(d):
        t = (place + d) % CHIPS
        return device(core, t // SIDE, t % SIDE, z)

    for d in range(1, MEMBERS):
        pl.semaphore_signal(barrier, inc=1, device_id=member_at(d), device_id_type=MESH)
    for d in range(1, CHIPS):
        pl.semaphore_signal(barrier, inc=1, device_id=place_at(d), device_id_type=MESH)

    def project(what, weight, total, cuts, also=None):
        for cut in cuts:
            begin, width, count = cut

            def step(k, carry):
                for one in (what, also) if also else (what,):
                    bring(one, cut, k).wait()
                at = pl.ds(pl.multiple_of(begin + k * width, width), width)
                total[...] += plain_dot(what[1][:, at], weight[:, at], BY_ROWS)
                return carry

            lax.fori_loop(0, count, step, 0)

    def clear(total):
        total[...] = jnp.zeros_like(total)

    def sides(in_total, out_total, lengths, count):
        slot = iota((LEN, 2 * RANK), 0)
        both = jnp.concatenate([in_total[...], out_total[...]], axis=1)
        both = [
            jnp.where(slot < lengths[e], both[e * LEN : (e + 1) * LEN], 0.0) for e in range(count)
        ]
        return jnp.concatenate(both, axis=0).T

    for total in (out_query, in_query, out_corpus, in_corpus):
        clear(total)
    project(qg, v_pout, out_query, OUT_CUTS, pout)
    project(qh, v_pin, in_query, QUERY_CUTS, pin)
    both = sides(in_query, out_query, query_lengths, queries)
    half = RANK // 2
    lower = iota((half, 2 * RANK), 1) < RANK
    mine = slabs.at[core, y, x, z]
    turned[pl.ds(0, queries * RANK), :] = gradients(both[RANK:], both[:RANK])
    for q in range(queries):
        even = turned[pl.ds(q * RANK, half, stride=2), :]
        odd = turned[pl.ds(q * RANK + 1, half, stride=2), :]
        mine[pl.ds(q * half, half), :] = jnp.where(lower, even, odd)

    pl.semaphore_wait(barrier, MEMBERS - 1 + CHIPS - 1)

    def block(p, places, whose=core):
        first, count, order = PARTS[p]
        index = [None] * 3
        for axis, place in zip(order, places):
            index[axis] = place
        return slabs.at[whose, index[0], index[1], index[2], pl.ds(first, count)]

    def own(p, phase, d=0):
        return (me[PARTS[p][2][phase]] + SIDE - d) % SIDE

    def to_axis(p, phase, ref, d, sem):
        there = list(me)
        axis = PARTS[p][2][phase]
        there[axis] = (there[axis] + d) % SIDE
        pltpu.make_async_remote_copy(
            src_ref=ref,
            dst_ref=ref,
            send_sem=slab_send.at[p, sem],
            recv_sem=slab_recv.at[p, sem],
            device_id=device(core, *there),
            device_id_type=MESH,
        ).start()

    def to_sibling(p, ref):
        pltpu.make_async_remote_copy(
            src_ref=ref,
            dst_ref=ref,
            send_sem=pair_send.at[p],
            recv_sem=pair_recv.at[p],
            device_id=device(1 - core, y, x, z),
            device_id_type=MESH,
        ).start()

    def wait_all(ref, sem):
        pltpu.make_async_copy(ref, ref, sem).wait()

    every = pl.ds(0, SIDE)
    others = pl.ds(0, SIDE - 1)

    def first_phase():
        for p in EVERYONE:
            ref = block(p, (own(p, 0), own(p, 1), own(p, 2)))
            for d in STEPS:
                to_axis(p, 0, ref, d, 0)

    def second_phase():
        for p in EVERYONE:
            wait_all(block(p, (others, 0, 0)), slab_recv.at[p, 0])
            ref = block(p, (every, own(p, 1), own(p, 2)))
            for d in STEPS:
                to_axis(p, 1, ref, d, d)
            for d in STEPS:
                to_axis(p, 2, ref, d, 3 + d)
            to_sibling(p, ref)

    def third_phase(d):
        for p in EVERYONE:
            ref = block(p, (every, own(p, 1, d), own(p, 2)))
            wait_all(ref, slab_recv.at[p, d])
            for far in STEPS:
                to_axis(p, 2, ref, far, 3 + far)
            to_sibling(p, ref)

    def last_phase(d):
        for p in EVERYONE:
            ref = block(p, (every, every, own(p, 2, d)))
            wait_all(ref, slab_recv.at[p, 3 + d])
            to_sibling(p, ref)

    first_phase()

    project(cg, v_pout, out_corpus, OUT_CUTS)
    project(ch, v_pin, in_corpus, CORPUS_CUTS[:1])
    second_phase()
    project(ch, v_pin, in_corpus, CORPUS_CUTS[1:])
    both = sides(in_corpus, out_corpus, corpus_lengths, examples)
    gram = plain_dot(left_of(both, 1), right_of(both, 1), BY_ROWS)
    lower = iota((RANK, 2 * RANK), 1) < RANK
    part[...] = jnp.where(lower, gram[:RANK], gram[RANK:])

    def octet(t):
        return pl.ds(pl.multiple_of(t * 8, 8), 8)

    def send_sum(stage, src, dst, to):
        pltpu.make_async_remote_copy(
            src_ref=src,
            dst_ref=dst,
            send_sem=sum_send.at[stage],
            recv_sem=sum_recv.at[stage],
            device_id=to,
            device_id_type=MESH,
        ).start()

    for d in range(1, MEMBERS):
        send_sum(0, part.at[octet((member + d) % MEMBERS)], from_members.at[d - 1], member_at(d))
    for d in STEPS:
        third_phase(d)
    for e in range(0, examples, 2):
        tokens = slice(e * LEN, (e + 2) * LEN)
        grads[pl.ds(e * RANK, 2 * RANK), :] = gradients(both[RANK:, tokens], both[:RANK, tokens])
    wait_all(from_members, sum_recv.at[0])
    total = part[octet(member), :]
    for d in range(MEMBERS - 1):
        total = total + from_members[d]
    piece[...] = total
    for d in range(1, CHIPS):
        send_sum(1, piece, from_plane.at[d - 1], place_at(d))
    last_phase(1)
    wait_all(from_plane, sum_recv.at[1])
    for d in range(CHIPS - 1):
        total = total + from_plane[d]
    fisher[octet(member), :] = total
    for d in range(1, MEMBERS):
        send_sum(2, fisher.at[octet(member)], fisher.at[octet(member)], member_at(d))

    for d in STEPS[1:]:
        last_phase(d)
    flat = slabs.reshape(DEVICES * SLAB, 2 * RANK)

    def halve(side, whose, i):
        chips = DEVICES // 2
        held = [
            flat[pl.ds(whose * chips * SLAB + q * half + i, chips, stride=SLAB), :] for q in range(queries)
        ]
        high, low = split(jnp.concatenate(held, axis=0).T)
        at = pl.ds(pl.multiple_of(i * 2 * RANK, 2 * RANK), 2 * RANK)
        q_high[at, pl.ds(side * DEVICES, DEVICES)] = high
        q_low[at, pl.ds(side * DEVICES, DEVICES)] = low

    def halve_side(side, whose):
        def some(b, carry):
            for k in range(16):
                halve(side, whose, b * 16 + k)
            return carry

        lax.fori_loop(0, half // 16, some, 0)

    halve_side(0, core)
    for p in EVERYONE:
        wait_all(block(p, (every, every, every), 0), pair_recv.at[p])
    halve_side(1, 1 - core)

    wait_all(from_members, sum_recv.at[2])
    pair = turned.at[pl.ds(0, RANK)]
    pair[...] = damp(fisher[...])
    invert_pair(pair)
    inverse = pair[...]
    swapped = pltpu.roll(inverse, RANK, 1)
    twice_in = right_of(jnp.where(lower, inverse, swapped), 0)
    lower = iota((examples * RANK, 2 * RANK), 1) < RANK
    held = grads[...]
    high = held.astype(BF16).astype(F32)
    thrice = jnp.concatenate([jnp.where(lower, high, held - high), high[:, :RANK]], axis=1)
    right_done = plain_dot(thrice.astype(BF16), twice_in, BY_COLUMNS)
    right_done = jnp.concatenate(
        [right_done[e * RANK : (e + 1) * RANK] for e in range(examples)], axis=1
    )
    lower = iota((RANK, 2 * RANK), 1) < RANK
    high = inverse.astype(BF16).astype(F32)
    swapped_high = pltpu.roll(high, RANK, 1)
    thrice = jnp.concatenate([jnp.where(lower, swapped_high, inverse - high), swapped_high[:, :RANK]], axis=1)
    done = plain_dot(thrice.astype(BF16), right_of(right_done, 0), BY_COLUMNS)
    for e in range(examples):
        turned[pl.ds(e * SLAB, RANK), :] = done[:, e * 2 * RANK : (e + 1) * 2 * RANK]
    lower = iota((examples, 2 * RANK), 1) < RANK
    left = jnp.concatenate(
        [
            jnp.where(
                lower,
                turned[pl.ds(i, examples, stride=SLAB), :],
                turned[pl.ds(i + 1, examples, stride=SLAB), :],
            )
            for i in range(0, RANK, 2)
        ],
        axis=1,
    )
    high = left.astype(BF16).astype(F32)
    ahead[...] = jnp.concatenate([high, left - high], axis=0).astype(BF16)

    left = ahead[...]
    main = plain_dot(left, q_high[...], BY_COLUMNS)
    rest = plain_dot(left, q_low[...], BY_COLUMNS)
    scores = main[:examples] + main[examples:] + rest[:examples]
    lane = iota((examples, DEVICES), 1)
    ours = lane // MEMBERS % 2 == core
    for h in range(queries):
        place_of = h * MEMBERS + lane // (2 * MEMBERS)
        held_at = lane % queries * (DEVICES // 2) + place_of * SIDE + lane // queries % SIDE
        picked = [
            jnp.take_along_axis(scores[:, k * DEVICES : (k + 1) * DEVICES], held_at, axis=1)
            for k in range(2)
        ]
        out[:, pl.ds(h * DEVICES, DEVICES)] = jnp.where(ours, picked[0], picked[1])

    for p in EVERYONE:
        wait_all(block(p, (others, 0, 0)), slab_send.at[p, 0])
        for d in STEPS:
            wait_all(block(p, (every, 0, 0)), slab_send.at[p, d])
            wait_all(block(p, (every, every, 0)), slab_send.at[p, 3 + d])
        wait_all(block(p, (every, every, every), 0), pair_send.at[p])
    wait_all(from_members, sum_send.at[0])
    wait_all(from_plane, sum_send.at[1])
    wait_all(from_members, sum_send.at[2])


def per_device(
    corpus_hidden,
    corpus_grad,
    corpus_lengths,
    query_hidden,
    query_grad,
    query_lengths,
    proj_in,
    proj_out,
):
    examples = corpus_hidden.shape[0]
    queries = query_hidden.shape[0]
    flat = lambda a: a.reshape(-1, a.shape[-1])
    anywhere = pl.BlockSpec(memory_space=pl.ANY)
    scalars = pl.BlockSpec(memory_space=pltpu.SMEM)
    operands = (
        flat(corpus_hidden),
        flat(corpus_grad),
        corpus_lengths,
        flat(query_hidden),
        flat(query_grad),
        query_lengths,
        proj_in.T,
        proj_out.T,
    )
    big = [operands[k] for k in (0, 1, 3, 4, 6, 7)]
    dma = pltpu.SemaphoreType.DMA
    steps = (proj_in.shape[0] + proj_out.shape[0]) // 1024
    scores = pl.pallas_call(
        kernel,
        out_shape=jax.ShapeDtypeStruct((examples, queries * DEVICES), F32),
        in_specs=[anywhere, anywhere, scalars, anywhere, anywhere, scalars, anywhere, anywhere],
        out_specs=pl.BlockSpec(memory_space=pltpu.VMEM),
        scratch_shapes=[pltpu.VMEM(a.shape, BF16) for a in big]
        + [
            pltpu.VMEM((examples * LEN, RANK), F32),
            pltpu.VMEM((examples * LEN, RANK), F32),
            pltpu.VMEM((queries * LEN, RANK), F32),
            pltpu.VMEM((queries * LEN, RANK), F32),
            pltpu.VMEM((examples * RANK, 2 * RANK), F32),
            pltpu.VMEM((2, SIDE, SIDE, SIDE, SLAB, 2 * RANK), F32),
            pltpu.VMEM((RANK * RANK, queries * DEVICES), BF16),
            pltpu.VMEM((RANK * RANK, queries * DEVICES), BF16),
            pltpu.VMEM((RANK, 2 * RANK), F32),
            pltpu.VMEM((8, 2 * RANK), F32),
            pltpu.VMEM((MEMBERS - 1, 8, 2 * RANK), F32),
            pltpu.VMEM((CHIPS - 1, 8, 2 * RANK), F32),
            pltpu.VMEM((RANK, 2 * RANK), F32),
            pltpu.VMEM((examples * SLAB, 2 * RANK), F32),
            pltpu.VMEM((2 * examples, RANK * RANK), BF16),
            dma((steps,)),
            dma((steps,)),
            dma((steps,)),
            dma((3,)),
            dma((3,)),
            dma((3, 7)),
            dma((3, 7)),
            dma((3,)),
            dma((3,)),
        ],
        compiler_params=pltpu.CompilerParams(
            collective_id=0, has_side_effects=True, vmem_limit_bytes=60 * 1024 * 1024
        ),
        name="influence",
    )(*operands)
    return scores


def solution(mesh):
    placed = (
        P(("corpus", "query"), None, None),
        P(("corpus", "query"), None, None),
        P(("corpus", "query")),
        P(("corpus", "query"), None, None),
        P(("corpus", "query"), None, None),
        P(("corpus", "query")),
        P(),
        P(),
    )
    return jax.shard_map(
        per_device,
        mesh=mesh,
        in_specs=placed,
        out_specs=P(("corpus", "query"), None),
        check_vma=False,
    )
```

```python
import jax
import jax.numpy as jnp
from jax import lax
from jax.experimental import pallas as pl
from jax.experimental.pallas import tpu as pltpu
from jax.sharding import PartitionSpec as P

F32 = jnp.float32
BF16 = jnp.bfloat16
MESH = pl.DeviceIdType.MESH
BY_ROWS = (((1,), (1,)), ((), ()))
BY_COLUMNS = (((1,), (0,)), ((), ()))

RANK = 64
LEN = 64
SIDE = 4
CHIPS = SIDE * SIDE
MEMBERS = 2 * SIDE
DEVICES = CHIPS * MEMBERS
SLAB = 72

PARTS = ((0, 24, (2, 1, 0)), (24, 24, (1, 0, 2)), (48, 16, (0, 2, 1)))
EVERYONE = range(len(PARTS))
STEPS = (1, 3, 2)


def coordinates():
    corpus = lax.axis_index("corpus")
    z = lax.axis_index("query")
    return corpus % 2, (corpus // 2) % SIDE, corpus // (2 * SIDE), z


def device(core, y, x, z):
    return ((y * SIDE + x) * 2 + core, z)


def iota(shape, axis):
    return lax.broadcasted_iota(jnp.int32, shape, axis)


def spread(block, row):
    return jnp.broadcast_to(block[row : row + 1], block.shape)


def plain_dot(a, b, dims):
    return lax.dot_general(a, b, dims, preferred_element_type=F32)


def damp(fisher):
    row, lane = iota(fisher.shape, 0), iota(fisher.shape, 1)
    diag = row == lane % RANK
    held = jnp.sum(jnp.where(diag, fisher, 0.0), axis=0, keepdims=True)
    lower = iota(held.shape, 1) < RANK
    trace_in = jnp.sum(jnp.where(lower, held, 0.0), axis=1, keepdims=True)
    trace_out = jnp.sum(jnp.where(lower, 0.0, held), axis=1, keepdims=True)
    shift = 0.1 / RANK * jnp.where(lower, trace_in, trace_out)
    return fisher + jnp.where(diag, shift, 0.0)


def invert_pair(pair):
    step = 8
    count = RANK // step
    shape = (step, 2 * RANK)
    lane, row = iota(shape, 1), iota(shape, 0)
    column = lane % RANK

    def eliminate(b, carry):
        first = pl.multiple_of(b * step, step)
        panel_at = pl.ds(first, step)
        offset = column - first
        inside = (offset >= 0) & (offset < step)
        where_j = [jnp.where(lane < RANK, 0, RANK) + first + j for j in range(step)]
        pick = lambda block: [jnp.take_along_axis(block, at, axis=1) for at in where_j]
        panel = pair[panel_at, :]
        picked = pick(panel)
        d = [[spread(picked[j], i) if j >= i else None for j in range(step)] for i in range(step)]
        r = [jnp.where(inside, jnp.where(offset == i, 1.0, 0.0), spread(panel, i)) for i in range(step)]
        for k in range(step):
            pivot = 1.0 / d[k][k]
            u = [None] * step
            for j in range(k + 1, step):
                u[j] = d[k][j] * pivot
            for i in range(k + 1, step):
                for j in range(i, step):
                    d[i][j] = d[i][j] - u[i] * d[k][j]
                r[i] = r[i] - u[i] * r[k]
            r[k] = r[k] * pivot
            for j in range(k + 1, step):
                d[k][j] = u[j]
        for k in range(step - 1, 0, -1):
            for i in range(k):
                r[i] = r[i] - d[i][k] * r[k]
        for o in range(count):
            at = pl.ds(o * step, step)
            block = pair[at, :]
            t = [c * rj for c, rj in zip(pick(block), r)]
            total = ((t[0] + t[1]) + (t[2] + t[3])) + ((t[4] + t[5]) + (t[6] + t[7]))
            pair[at, :] = jnp.where(inside, 0.0, block) - total
        block = r[0]
        for i in range(1, step):
            block = jnp.where(row == i, r[i], block)
        pair[panel_at, :] = block
        return carry

    lax.fori_loop(0, count, eliminate, 0)


def split(values):
    high = values.astype(BF16)
    low = (values - high.astype(F32)).astype(BF16)
    return high, low


def left_of(values, axis):
    high, low = split(values)
    return jnp.concatenate([high, low, high], axis=axis)


def right_of(values, axis):
    high, low = split(values)
    return jnp.concatenate([high, high, low], axis=axis)


def gradients(out_side, in_side):
    lower = iota(out_side.shape, 1) < LEN
    left = jnp.concatenate(
        [left_of(jnp.where(lower, out_side, 0.0), 1), left_of(jnp.where(lower, 0.0, out_side), 1)], axis=0
    )
    right = right_of(in_side, 1)
    return plain_dot(left, jnp.concatenate([right, right], axis=0), BY_ROWS)


OUT_CUTS = ((0, 4096, 1),)
QUERY_CUTS = ((0, 3584, 4),)
CORPUS_CUTS = ((0, 4096, 1), (4096, 4096, 2), (12288, 2048, 1))


def kernel(
    corpus_hidden,
    corpus_grad,
    corpus_lengths,
    query_hidden,
    query_grad,
    query_lengths,
    proj_in,
    proj_out,
    out,
    v_ch,
    v_cg,
    v_qh,
    v_qg,
    v_pin,
    v_pout,
    in_corpus,
    out_corpus,
    in_query,
    out_query,
    grads,
    slabs,
    q_high,
    q_low,
    part,
    piece,
    from_members,
    from_plane,
    fisher,
    turned,
    ahead,
    query_sem,
    corpus_sem,
    weight_sem,
    sum_send,
    sum_recv,
    slab_send,
    slab_recv,
    pair_send,
    pair_recv,
):
    core, x, y, z = coordinates()
    me = (y, x, z)
    member, place = core * SIDE + z, y * SIDE + x
    examples = corpus_hidden.shape[0] // LEN
    queries = query_hidden.shape[0] // LEN

    def bring(one, cut, k):
        src, dst, sem, first = one
        begin, width, _ = cut
        at = pl.ds(pl.multiple_of(begin + k * width, width), width)
        return pltpu.make_async_copy(src.at[:, at], dst.at[:, at], sem.at[first + begin // 1024 + k])

    def bring_all(cuts, *what):
        for cut in cuts:

            def start(k, carry):
                for one in what:
                    bring(one, cut, k).start()
                return carry

            lax.fori_loop(0, cut[2], start, 0)

    last = proj_in.shape[1] // 1024
    pout = (proj_out, v_pout, weight_sem, last)
    pin = (proj_in, v_pin, weight_sem, 0)
    qg = (query_grad, v_qg, query_sem, last)
    qh = (query_hidden, v_qh, query_sem, 0)
    cg = (corpus_grad, v_cg, corpus_sem, last)
    ch = (corpus_hidden, v_ch, corpus_sem, 0)
    bring_all(OUT_CUTS, pout, qg)
    bring_all(QUERY_CUTS, pin, qh)
    bring_all(OUT_CUTS, cg)
    bring_all(CORPUS_CUTS, ch)

    barrier = pltpu.get_barrier_semaphore()

    def member_at(d):
        t = (member + d) % MEMBERS
        return device(t // SIDE, y, x, t % SIDE)

    def place_at(d):
        t = (place + d) % CHIPS
        return device(core, t // SIDE, t % SIDE, z)

    for d in range(1, MEMBERS):
        pl.semaphore_signal(barrier, inc=1, device_id=member_at(d), device_id_type=MESH)
    for d in range(1, CHIPS):
        pl.semaphore_signal(barrier, inc=1, device_id=place_at(d), device_id_type=MESH)

    def project(what, weight, total, cuts, also=None):
        for cut in cuts:
            begin, width, count = cut

            def step(k, carry):
                for one in (what, also) if also else (what,):
                    bring(one, cut, k).wait()
                at = pl.ds(pl.multiple_of(begin + k * width, width), width)
                total[...] += plain_dot(what[1][:, at], weight[:, at], BY_ROWS)
                return carry

            lax.fori_loop(0, count, step, 0)

    def clear(total):
        total[...] = jnp.zeros_like(total)

    def sides(in_total, out_total, lengths, count):
        slot = iota((LEN, 2 * RANK), 0)
        both = jnp.concatenate([in_total[...], out_total[...]], axis=1)
        both = [
            jnp.where(slot < lengths[e], both[e * LEN : (e + 1) * LEN], 0.0) for e in range(count)
        ]
        return jnp.concatenate(both, axis=0).T

    for total in (out_query, in_query, out_corpus, in_corpus):
        clear(total)
    project(qg, v_pout, out_query, OUT_CUTS, pout)
    project(qh, v_pin, in_query, QUERY_CUTS, pin)
    both = sides(in_query, out_query, query_lengths, queries)
    half = RANK // 2
    lower = iota((half, 2 * RANK), 1) < RANK
    mine = slabs.at[core, y, x, z]
    turned[pl.ds(0, queries * RANK), :] = gradients(both[RANK:], both[:RANK])
    for q in range(queries):
        even = turned[pl.ds(q * RANK, half, stride=2), :]
        odd = turned[pl.ds(q * RANK + 1, half, stride=2), :]
        mine[pl.ds(q * half, half), :] = jnp.where(lower, even, odd)

    pl.semaphore_wait(barrier, MEMBERS - 1 + CHIPS - 1)

    def block(p, places, whose=core):
        first, count, order = PARTS[p]
        index = [None] * 3
        for axis, place in zip(order, places):
            index[axis] = place
        return slabs.at[whose, index[0], index[1], index[2], pl.ds(first, count)]

    def own(p, phase, d=0):
        return (me[PARTS[p][2][phase]] + SIDE - d) % SIDE

    def to_axis(p, phase, ref, d, sem):
        there = list(me)
        axis = PARTS[p][2][phase]
        there[axis] = (there[axis] + d) % SIDE
        pltpu.make_async_remote_copy(
            src_ref=ref,
            dst_ref=ref,
            send_sem=slab_send.at[p, sem],
            recv_sem=slab_recv.at[p, sem],
            device_id=device(core, *there),
            device_id_type=MESH,
        ).start()

    def to_sibling(p, ref):
        pltpu.make_async_remote_copy(
            src_ref=ref,
            dst_ref=ref,
            send_sem=pair_send.at[p],
            recv_sem=pair_recv.at[p],
            device_id=device(1 - core, y, x, z),
            device_id_type=MESH,
        ).start()

    def wait_all(ref, sem):
        pltpu.make_async_copy(ref, ref, sem).wait()

    every = pl.ds(0, SIDE)
    others = pl.ds(0, SIDE - 1)

    def first_phase():
        for p in EVERYONE:
            ref = block(p, (own(p, 0), own(p, 1), own(p, 2)))
            for d in STEPS:
                to_axis(p, 0, ref, d, 0)

    def second_phase():
        for p in EVERYONE:
            wait_all(block(p, (others, 0, 0)), slab_recv.at[p, 0])
            ref = block(p, (every, own(p, 1), own(p, 2)))
            for d in STEPS:
                to_axis(p, 1, ref, d, d)
            for d in STEPS:
                to_axis(p, 2, ref, d, 3 + d)
            to_sibling(p, ref)

    def third_phase(d):
        for p in EVERYONE:
            ref = block(p, (every, own(p, 1, d), own(p, 2)))
            wait_all(ref, slab_recv.at[p, d])
            for far in STEPS:
                to_axis(p, 2, ref, far, 3 + far)
            to_sibling(p, ref)

    def last_phase(d):
        for p in EVERYONE:
            ref = block(p, (every, every, own(p, 2, d)))
            wait_all(ref, slab_recv.at[p, 3 + d])
            to_sibling(p, ref)

    first_phase()

    project(cg, v_pout, out_corpus, OUT_CUTS)
    project(ch, v_pin, in_corpus, CORPUS_CUTS[:1])
    second_phase()
    project(ch, v_pin, in_corpus, CORPUS_CUTS[1:])
    both = sides(in_corpus, out_corpus, corpus_lengths, examples)
    gram = plain_dot(left_of(both, 1), right_of(both, 1), BY_ROWS)
    lower = iota((RANK, 2 * RANK), 1) < RANK
    part[...] = jnp.where(lower, gram[:RANK], gram[RANK:])

    def octet(t):
        return pl.ds(pl.multiple_of(t * 8, 8), 8)

    def send_sum(stage, src, dst, to):
        pltpu.make_async_remote_copy(
            src_ref=src,
            dst_ref=dst,
            send_sem=sum_send.at[stage],
            recv_sem=sum_recv.at[stage],
            device_id=to,
            device_id_type=MESH,
        ).start()

    for d in range(1, MEMBERS):
        send_sum(0, part.at[octet((member + d) % MEMBERS)], from_members.at[d - 1], member_at(d))
    for d in STEPS[:2]:
        third_phase(d)
    for e in range(0, examples, 2):
        tokens = slice(e * LEN, (e + 2) * LEN)
        grads[pl.ds(e * RANK, 2 * RANK), :] = gradients(both[RANK:, tokens], both[:RANK, tokens])
    wait_all(from_members, sum_recv.at[0])
    total = part[octet(member), :]
    for d in range(MEMBERS - 1):
        total = total + from_members[d]
    piece[...] = total
    for d in range(1, CHIPS):
        send_sum(1, piece, from_plane.at[d - 1], place_at(d))
    third_phase(STEPS[2])
    wait_all(from_plane, sum_recv.at[1])
    for d in range(CHIPS - 1):
        total = total + from_plane[d]
    fisher[octet(member), :] = total
    for d in range(1, MEMBERS):
        send_sum(2, fisher.at[octet(member)], fisher.at[octet(member)], member_at(d))

    for d in STEPS:
        last_phase(d)
    flat = slabs.reshape(DEVICES * SLAB, 2 * RANK)

    def halve(side, whose, i):
        chips = DEVICES // 2
        held = [
            flat[pl.ds(whose * chips * SLAB + q * half + i, chips, stride=SLAB), :] for q in range(queries)
        ]
        high, low = split(jnp.concatenate(held, axis=0).T)
        at = pl.ds(pl.multiple_of(i * 2 * RANK, 2 * RANK), 2 * RANK)
        q_high[at, pl.ds(side * DEVICES, DEVICES)] = high
        q_low[at, pl.ds(side * DEVICES, DEVICES)] = low

    def halve_side(side, whose):
        def some(b, carry):
            for k in range(16):
                halve(side, whose, b * 16 + k)
            return carry

        lax.fori_loop(0, half // 16, some, 0)

    halve_side(0, core)

    wait_all(from_members, sum_recv.at[2])
    pair = turned.at[pl.ds(0, RANK)]
    pair[...] = damp(fisher[...])
    invert_pair(pair)
    for p in EVERYONE:
        wait_all(block(p, (every, every, every), 0), pair_recv.at[p])
    halve_side(1, 1 - core)
    inverse = pair[...]
    swapped = pltpu.roll(inverse, RANK, 1)
    twice_in = right_of(jnp.where(lower, inverse, swapped), 0)
    lower = iota((examples * RANK, 2 * RANK), 1) < RANK
    held = grads[...]
    high = held.astype(BF16).astype(F32)
    thrice = jnp.concatenate([jnp.where(lower, high, held - high), high[:, :RANK]], axis=1)
    right_done = plain_dot(thrice.astype(BF16), twice_in, BY_COLUMNS)
    right_done = jnp.concatenate(
        [right_done[e * RANK : (e + 1) * RANK] for e in range(examples)], axis=1
    )
    lower = iota((RANK, 2 * RANK), 1) < RANK
    high = inverse.astype(BF16).astype(F32)
    swapped_high = pltpu.roll(high, RANK, 1)
    thrice = jnp.concatenate([jnp.where(lower, swapped_high, inverse - high), swapped_high[:, :RANK]], axis=1)
    done = plain_dot(thrice.astype(BF16), right_of(right_done, 0), BY_COLUMNS)
    for e in range(examples):
        turned[pl.ds(e * SLAB, RANK), :] = done[:, e * 2 * RANK : (e + 1) * 2 * RANK]
    lower = iota((examples, 2 * RANK), 1) < RANK
    left = jnp.concatenate(
        [
            jnp.where(
                lower,
                turned[pl.ds(i, examples, stride=SLAB), :],
                turned[pl.ds(i + 1, examples, stride=SLAB), :],
            )
            for i in range(0, RANK, 2)
        ],
        axis=1,
    )
    high = left.astype(BF16).astype(F32)
    ahead[...] = jnp.concatenate([high, left - high], axis=0).astype(BF16)

    left = ahead[...]
    main = plain_dot(left, q_high[...], BY_COLUMNS)
    rest = plain_dot(left, q_low[...], BY_COLUMNS)
    scores = main[:examples] + main[examples:] + rest[:examples]
    lane = iota((examples, DEVICES), 1)
    ours = lane // MEMBERS % 2 == core
    for h in range(queries):
        place_of = h * MEMBERS + lane // (2 * MEMBERS)
        held_at = lane % queries * (DEVICES // 2) + place_of * SIDE + lane // queries % SIDE
        picked = [
            jnp.take_along_axis(scores[:, k * DEVICES : (k + 1) * DEVICES], held_at, axis=1)
            for k in range(2)
        ]
        out[:, pl.ds(h * DEVICES, DEVICES)] = jnp.where(ours, picked[0], picked[1])

    for p in EVERYONE:
        wait_all(block(p, (others, 0, 0)), slab_send.at[p, 0])
        for d in STEPS:
            wait_all(block(p, (every, 0, 0)), slab_send.at[p, d])
            wait_all(block(p, (every, every, 0)), slab_send.at[p, 3 + d])
        wait_all(block(p, (every, every, every), 0), pair_send.at[p])
    wait_all(from_members, sum_send.at[0])
    wait_all(from_plane, sum_send.at[1])
    wait_all(from_members, sum_send.at[2])


def per_device(
    corpus_hidden,
    corpus_grad,
    corpus_lengths,
    query_hidden,
    query_grad,
    query_lengths,
    proj_in,
    proj_out,
):
    examples = corpus_hidden.shape[0]
    queries = query_hidden.shape[0]
    flat = lambda a: a.reshape(-1, a.shape[-1])
    anywhere = pl.BlockSpec(memory_space=pl.ANY)
    scalars = pl.BlockSpec(memory_space=pltpu.SMEM)
    operands = (
        flat(corpus_hidden),
        flat(corpus_grad),
        corpus_lengths,
        flat(query_hidden),
        flat(query_grad),
        query_lengths,
        proj_in.T,
        proj_out.T,
    )
    big = [operands[k] for k in (0, 1, 3, 4, 6, 7)]
    dma = pltpu.SemaphoreType.DMA
    steps = (proj_in.shape[0] + proj_out.shape[0]) // 1024
    scores = pl.pallas_call(
        kernel,
        out_shape=pltpu.VMEM((examples, queries * DEVICES), F32),
        in_specs=[anywhere, anywhere, scalars, anywhere, anywhere, scalars, anywhere, anywhere],
        out_specs=pl.BlockSpec(memory_space=pltpu.VMEM),
        scratch_shapes=[pltpu.VMEM(a.shape, BF16) for a in big]
        + [
            pltpu.VMEM((examples * LEN, RANK), F32),
            pltpu.VMEM((examples * LEN, RANK), F32),
            pltpu.VMEM((queries * LEN, RANK), F32),
            pltpu.VMEM((queries * LEN, RANK), F32),
            pltpu.VMEM((examples * RANK, 2 * RANK), F32),
            pltpu.VMEM((2, SIDE, SIDE, SIDE, SLAB, 2 * RANK), F32),
            pltpu.VMEM((RANK * RANK, queries * DEVICES), BF16),
            pltpu.VMEM((RANK * RANK, queries * DEVICES), BF16),
            pltpu.VMEM((RANK, 2 * RANK), F32),
            pltpu.VMEM((8, 2 * RANK), F32),
            pltpu.VMEM((MEMBERS - 1, 8, 2 * RANK), F32),
            pltpu.VMEM((CHIPS - 1, 8, 2 * RANK), F32),
            pltpu.VMEM((RANK, 2 * RANK), F32),
            pltpu.VMEM((examples * SLAB, 2 * RANK), F32),
            pltpu.VMEM((2 * examples, RANK * RANK), BF16),
            dma((steps,)),
            dma((steps,)),
            dma((steps,)),
            dma((3,)),
            dma((3,)),
            dma((3, 7)),
            dma((3, 7)),
            dma((3,)),
            dma((3,)),
        ],
        compiler_params=pltpu.CompilerParams(
            collective_id=0, has_side_effects=True, vmem_limit_bytes=60 * 1024 * 1024
        ),
        name="influence",
    )(*operands)
    return scores


def solution(mesh):
    placed = (
        P(("corpus", "query"), None, None),
        P(("corpus", "query"), None, None),
        P(("corpus", "query")),
        P(("corpus", "query"), None, None),
        P(("corpus", "query"), None, None),
        P(("corpus", "query")),
        P(),
        P(),
    )
    return jax.shard_map(
        per_device,
        mesh=mesh,
        in_specs=placed,
        out_specs=P(("corpus", "query"), None),
        check_vma=False,
    )
```

```python
import jax
import jax.numpy as jnp
from jax import lax
from jax.experimental import pallas as pl
from jax.experimental.pallas import tpu as pltpu
from jax.sharding import PartitionSpec as P

F32 = jnp.float32
BF16 = jnp.bfloat16
MESH = pl.DeviceIdType.MESH
BY_ROWS = (((1,), (1,)), ((), ()))
BY_COLUMNS = (((1,), (0,)), ((), ()))

RANK = 64
LEN = 64
SIDE = 4
CHIPS = SIDE * SIDE
MEMBERS = 2 * SIDE
DEVICES = CHIPS * MEMBERS
SLAB = 72

PARTS = ((0, 24, (2, 1, 0)), (24, 24, (1, 0, 2)), (48, 16, (0, 2, 1)))
EVERYONE = range(len(PARTS))
STEPS = (1, 3, 2)


def coordinates():
    corpus = lax.axis_index("corpus")
    z = lax.axis_index("query")
    return corpus % 2, (corpus // 2) % SIDE, corpus // (2 * SIDE), z


def device(core, y, x, z):
    return ((y * SIDE + x) * 2 + core, z)


def iota(shape, axis):
    return lax.broadcasted_iota(jnp.int32, shape, axis)


def spread(block, row):
    return jnp.broadcast_to(block[row : row + 1], block.shape)


def plain_dot(a, b, dims):
    return lax.dot_general(a, b, dims, preferred_element_type=F32)


def damp(fisher):
    row, lane = iota(fisher.shape, 0), iota(fisher.shape, 1)
    diag = row == lane % RANK
    held = jnp.sum(jnp.where(diag, fisher, 0.0), axis=0, keepdims=True)
    lower = iota(held.shape, 1) < RANK
    trace_in = jnp.sum(jnp.where(lower, held, 0.0), axis=1, keepdims=True)
    trace_out = jnp.sum(jnp.where(lower, 0.0, held), axis=1, keepdims=True)
    shift = 0.1 / RANK * jnp.where(lower, trace_in, trace_out)
    return fisher + jnp.where(diag, shift, 0.0)


def invert_pair(pair):
    step = 8
    count = RANK // step
    shape = (step, 2 * RANK)
    lane, row = iota(shape, 1), iota(shape, 0)
    column = lane % RANK

    def eliminate(b, carry):
        first = pl.multiple_of(b * step, step)
        panel_at = pl.ds(first, step)
        offset = column - first
        inside = (offset >= 0) & (offset < step)
        where_j = [jnp.where(lane < RANK, 0, RANK) + first + j for j in range(step)]
        pick = lambda block: [jnp.take_along_axis(block, at, axis=1) for at in where_j]
        panel = pair[panel_at, :]
        picked = pick(panel)
        d = [[spread(picked[j], i) if j >= i else None for j in range(step)] for i in range(step)]
        r = [jnp.where(inside, jnp.where(offset == i, 1.0, 0.0), spread(panel, i)) for i in range(step)]
        for k in range(step):
            pivot = 1.0 / d[k][k]
            u = [None] * step
            for j in range(k + 1, step):
                u[j] = d[k][j] * pivot
            for i in range(k + 1, step):
                for j in range(i, step):
                    d[i][j] = d[i][j] - u[i] * d[k][j]
                r[i] = r[i] - u[i] * r[k]
            r[k] = r[k] * pivot
            for j in range(k + 1, step):
                d[k][j] = u[j]
        for k in range(step - 1, 0, -1):
            for i in range(k):
                r[i] = r[i] - d[i][k] * r[k]
        for o in range(count):
            at = pl.ds(o * step, step)
            block = pair[at, :]
            t = [c * rj for c, rj in zip(pick(block), r)]
            total = ((t[0] + t[1]) + (t[2] + t[3])) + ((t[4] + t[5]) + (t[6] + t[7]))
            pair[at, :] = jnp.where(inside, 0.0, block) - total
        block = r[0]
        for i in range(1, step):
            block = jnp.where(row == i, r[i], block)
        pair[panel_at, :] = block
        return carry

    lax.fori_loop(0, count, eliminate, 0)


def split(values):
    high = values.astype(BF16)
    low = (values - high.astype(F32)).astype(BF16)
    return high, low


def left_of(values, axis):
    high, low = split(values)
    return jnp.concatenate([high, low, high], axis=axis)


def right_of(values, axis):
    high, low = split(values)
    return jnp.concatenate([high, high, low], axis=axis)


def gradients(out_side, in_side):
    lower = iota(out_side.shape, 1) < LEN
    left = jnp.concatenate(
        [left_of(jnp.where(lower, out_side, 0.0), 1), left_of(jnp.where(lower, 0.0, out_side), 1)], axis=0
    )
    right = right_of(in_side, 1)
    return plain_dot(left, jnp.concatenate([right, right], axis=0), BY_ROWS)


OUT_CUTS = ((0, 4096, 1),)
QUERY_CUTS = ((0, 3584, 4),)
CORPUS_CUTS = ((0, 4096, 1), (4096, 4096, 2), (12288, 2048, 1))


def kernel(
    corpus_hidden,
    corpus_grad,
    corpus_lengths,
    query_hidden,
    query_grad,
    query_lengths,
    proj_in,
    proj_out,
    out,
    v_ch,
    v_cg,
    v_qh,
    v_qg,
    v_pin,
    v_pout,
    in_corpus,
    out_corpus,
    in_query,
    out_query,
    grads,
    slabs,
    q_high,
    q_low,
    part,
    piece,
    from_members,
    from_plane,
    fisher,
    turned,
    ahead,
    query_sem,
    corpus_sem,
    weight_sem,
    sum_send,
    sum_recv,
    slab_send,
    slab_recv,
    pair_send,
    pair_recv,
):
    core, x, y, z = coordinates()
    me = (y, x, z)
    member, place = core * SIDE + z, y * SIDE + x
    examples = corpus_hidden.shape[0] // LEN
    queries = query_hidden.shape[0] // LEN

    def bring(one, cut, k):
        src, dst, sem, first = one
        begin, width, _ = cut
        at = pl.ds(pl.multiple_of(begin + k * width, width), width)
        return pltpu.make_async_copy(src.at[:, at], dst.at[:, at], sem.at[first + begin // 1024 + k])

    def bring_all(cuts, *what):
        for cut in cuts:

            def start(k, carry):
                for one in what:
                    bring(one, cut, k).start()
                return carry

            lax.fori_loop(0, cut[2], start, 0)

    last = proj_in.shape[1] // 1024
    pout = (proj_out, v_pout, weight_sem, last)
    pin = (proj_in, v_pin, weight_sem, 0)
    qg = (query_grad, v_qg, query_sem, last)
    qh = (query_hidden, v_qh, query_sem, 0)
    cg = (corpus_grad, v_cg, corpus_sem, last)
    ch = (corpus_hidden, v_ch, corpus_sem, 0)
    bring_all(OUT_CUTS, pout, qg)
    bring_all(QUERY_CUTS, pin, qh)
    bring_all(OUT_CUTS, cg)
    bring_all(CORPUS_CUTS, ch)

    barrier = pltpu.get_barrier_semaphore()

    def member_at(d):
        t = (member + d) % MEMBERS
        return device(t // SIDE, y, x, t % SIDE)

    def place_at(d):
        t = (place + d) % CHIPS
        return device(core, t // SIDE, t % SIDE, z)

    for d in range(1, MEMBERS):
        pl.semaphore_signal(barrier, inc=1, device_id=member_at(d), device_id_type=MESH)
    for d in range(1, CHIPS):
        pl.semaphore_signal(barrier, inc=1, device_id=place_at(d), device_id_type=MESH)

    def project(what, weight, total, cuts, also=None):
        for cut in cuts:
            begin, width, count = cut

            def step(k, carry):
                for one in (what, also) if also else (what,):
                    bring(one, cut, k).wait()
                at = pl.ds(pl.multiple_of(begin + k * width, width), width)
                total[...] += plain_dot(what[1][:, at], weight[:, at], BY_ROWS)
                return carry

            lax.fori_loop(0, count, step, 0)

    def clear(total):
        total[...] = jnp.zeros_like(total)

    def sides(in_total, out_total, lengths, count):
        slot = iota((LEN, 2 * RANK), 0)
        both = jnp.concatenate([in_total[...], out_total[...]], axis=1)
        both = [
            jnp.where(slot < lengths[e], both[e * LEN : (e + 1) * LEN], 0.0) for e in range(count)
        ]
        return jnp.concatenate(both, axis=0).T

    for total in (out_query, in_query, out_corpus, in_corpus):
        clear(total)
    project(qg, v_pout, out_query, OUT_CUTS, pout)
    project(qh, v_pin, in_query, QUERY_CUTS, pin)
    both = sides(in_query, out_query, query_lengths, queries)
    half = RANK // 2
    lower = iota((half, 2 * RANK), 1) < RANK
    mine = slabs.at[core, y, x, z]
    turned[pl.ds(0, queries * RANK), :] = gradients(both[RANK:], both[:RANK])
    for q in range(queries):
        even = turned[pl.ds(q * RANK, half, stride=2), :]
        odd = turned[pl.ds(q * RANK + 1, half, stride=2), :]
        mine[pl.ds(q * half, half), :] = jnp.where(lower, even, odd)

    pl.semaphore_wait(barrier, MEMBERS - 1 + CHIPS - 1)

    def block(p, places, whose=core):
        first, count, order = PARTS[p]
        index = [None] * 3
        for axis, place in zip(order, places):
            index[axis] = place
        return slabs.at[whose, index[0], index[1], index[2], pl.ds(first, count)]

    def own(p, phase, d=0):
        return (me[PARTS[p][2][phase]] + SIDE - d) % SIDE

    def to_axis(p, phase, ref, d, sem):
        there = list(me)
        axis = PARTS[p][2][phase]
        there[axis] = (there[axis] + d) % SIDE
        pltpu.make_async_remote_copy(
            src_ref=ref,
            dst_ref=ref,
            send_sem=slab_send.at[p, sem],
            recv_sem=slab_recv.at[p, sem],
            device_id=device(core, *there),
            device_id_type=MESH,
        ).start()

    def to_sibling(p, ref):
        pltpu.make_async_remote_copy(
            src_ref=ref,
            dst_ref=ref,
            send_sem=pair_send.at[p],
            recv_sem=pair_recv.at[p],
            device_id=device(1 - core, y, x, z),
            device_id_type=MESH,
        ).start()

    def wait_all(ref, sem):
        pltpu.make_async_copy(ref, ref, sem).wait()

    every = pl.ds(0, SIDE)
    others = pl.ds(0, SIDE - 1)

    def first_phase():
        for p in EVERYONE:
            ref = block(p, (own(p, 0), own(p, 1), own(p, 2)))
            for d in STEPS:
                to_axis(p, 0, ref, d, 0)

    def second_phase():
        for p in EVERYONE:
            wait_all(block(p, (others, 0, 0)), slab_recv.at[p, 0])
            ref = block(p, (every, own(p, 1), own(p, 2)))
            for d in STEPS:
                to_axis(p, 1, ref, d, d)
            for d in STEPS:
                to_axis(p, 2, ref, d, 3 + d)
            to_sibling(p, ref)

    def third_phase(d):
        for p in EVERYONE:
            ref = block(p, (every, own(p, 1, d), own(p, 2)))
            wait_all(ref, slab_recv.at[p, d])
            for far in STEPS:
                to_axis(p, 2, ref, far, 3 + far)
            to_sibling(p, ref)

    def last_phase(d):
        for p in EVERYONE:
            ref = block(p, (every, every, own(p, 2, d)))
            wait_all(ref, slab_recv.at[p, 3 + d])
            to_sibling(p, ref)

    first_phase()

    project(cg, v_pout, out_corpus, OUT_CUTS)
    project(ch, v_pin, in_corpus, CORPUS_CUTS[:1])
    second_phase()
    project(ch, v_pin, in_corpus, CORPUS_CUTS[1:])
    both = sides(in_corpus, out_corpus, corpus_lengths, examples)
    gram = plain_dot(left_of(both, 1), right_of(both, 1), BY_ROWS)
    lower = iota((RANK, 2 * RANK), 1) < RANK
    part[...] = jnp.where(lower, gram[:RANK], gram[RANK:])

    def octet(t):
        return pl.ds(pl.multiple_of(t * 8, 8), 8)

    def send_sum(stage, src, dst, to):
        pltpu.make_async_remote_copy(
            src_ref=src,
            dst_ref=dst,
            send_sem=sum_send.at[stage],
            recv_sem=sum_recv.at[stage],
            device_id=to,
            device_id_type=MESH,
        ).start()

    for d in range(1, MEMBERS):
        send_sum(0, part.at[octet((member + d) % MEMBERS)], from_members.at[d - 1], member_at(d))
    third_phase(STEPS[0])
    for e in range(0, examples, 2):
        tokens = slice(e * LEN, (e + 2) * LEN)
        grads[pl.ds(e * RANK, 2 * RANK), :] = gradients(both[RANK:, tokens], both[:RANK, tokens])
    wait_all(from_members, sum_recv.at[0])
    total = part[octet(member), :]
    for d in range(MEMBERS - 1):
        total = total + from_members[d]
    piece[...] = total
    for d in range(1, CHIPS):
        send_sum(1, piece, from_plane.at[d - 1], place_at(d))
    for d in STEPS[1:]:
        third_phase(d)
    wait_all(from_plane, sum_recv.at[1])
    for d in range(CHIPS - 1):
        total = total + from_plane[d]
    fisher[octet(member), :] = total
    for d in range(1, MEMBERS):
        send_sum(2, fisher.at[octet(member)], fisher.at[octet(member)], member_at(d))

    for d in STEPS:
        last_phase(d)
    flat = slabs.reshape(3 * DEVICES // 2 * SLAB, 2 * RANK)

    def halve(side, whose, i):
        chips = DEVICES // 2
        held = [
            flat[pl.ds(whose * chips * SLAB + q * half + i, chips, stride=SLAB), :] for q in range(queries)
        ]
        high, low = split(jnp.concatenate(held, axis=0).T)
        at = pl.ds(pl.multiple_of(i * 2 * RANK, 2 * RANK), 2 * RANK)
        q_high[at, pl.ds(side * DEVICES, DEVICES)] = high
        q_low[at, pl.ds(side * DEVICES, DEVICES)] = low

    def halve_side(side, whose):
        def some(b, carry):
            for k in range(16):
                halve(side, whose, b * 16 + k)
            return carry

        lax.fori_loop(0, half // 16, some, 0)

    halve_side(0, core)

    wait_all(from_members, sum_recv.at[2])
    pair = turned.at[pl.ds(0, RANK)]
    pair[...] = damp(fisher[...])
    invert_pair(pair)
    for p in EVERYONE:
        wait_all(block(p, (every, every, every), 0), pair_recv.at[p])
    halve_side(1, 1 - core)
    inverse = pair[...]
    swapped = pltpu.roll(inverse, RANK, 1)
    twice_in = right_of(jnp.where(lower, inverse, swapped), 0)
    lower = iota((examples * RANK, 2 * RANK), 1) < RANK
    held = grads[...]
    high = held.astype(BF16).astype(F32)
    thrice = jnp.concatenate([jnp.where(lower, high, held - high), high[:, :RANK]], axis=1)
    right_done = plain_dot(thrice.astype(BF16), twice_in, BY_COLUMNS)
    right_done = jnp.concatenate(
        [right_done[e * RANK : (e + 1) * RANK] for e in range(examples)], axis=1
    )
    lower = iota((RANK, 2 * RANK), 1) < RANK
    high = inverse.astype(BF16).astype(F32)
    swapped_high = pltpu.roll(high, RANK, 1)
    thrice = jnp.concatenate([jnp.where(lower, swapped_high, inverse - high), swapped_high[:, :RANK]], axis=1)
    done = plain_dot(thrice.astype(BF16), right_of(right_done, 0), BY_COLUMNS)
    for e in range(examples):
        turned[pl.ds(e * SLAB, RANK), :] = done[:, e * 2 * RANK : (e + 1) * 2 * RANK]
    lower = iota((examples, 2 * RANK), 1) < RANK
    left = jnp.concatenate(
        [
            jnp.where(
                lower,
                turned[pl.ds(i, examples, stride=SLAB), :],
                turned[pl.ds(i + 1, examples, stride=SLAB), :],
            )
            for i in range(0, RANK, 2)
        ],
        axis=1,
    )
    high = left.astype(BF16).astype(F32)
    ahead[...] = jnp.concatenate([high, left - high], axis=0).astype(BF16)

    left = ahead[...]
    main = plain_dot(left, q_high[...], BY_COLUMNS)
    rest = plain_dot(left, q_low[...], BY_COLUMNS)
    scores = main[:examples] + main[examples:] + rest[:examples]
    lane = iota((examples, DEVICES), 1)
    ours = lane // MEMBERS % 2 == core
    for h in range(queries):
        place_of = h * MEMBERS + lane // (2 * MEMBERS)
        held_at = lane % queries * (DEVICES // 2) + place_of * SIDE + lane // queries % SIDE
        picked = [
            jnp.take_along_axis(scores[:, k * DEVICES : (k + 1) * DEVICES], held_at, axis=1)
            for k in range(2)
        ]
        out[:, pl.ds(h * DEVICES, DEVICES)] = jnp.where(ours, picked[0], picked[1])

    for p in EVERYONE:
        wait_all(block(p, (others, 0, 0)), slab_send.at[p, 0])
        for d in STEPS:
            wait_all(block(p, (every, 0, 0)), slab_send.at[p, d])
            wait_all(block(p, (every, every, 0)), slab_send.at[p, 3 + d])
        wait_all(block(p, (every, every, every), 0), pair_send.at[p])
    wait_all(from_members, sum_send.at[0])
    wait_all(from_plane, sum_send.at[1])
    wait_all(from_members, sum_send.at[2])


def per_device(
    corpus_hidden,
    corpus_grad,
    corpus_lengths,
    query_hidden,
    query_grad,
    query_lengths,
    proj_in,
    proj_out,
):
    examples = corpus_hidden.shape[0]
    queries = query_hidden.shape[0]
    flat = lambda a: a.reshape(-1, a.shape[-1])
    anywhere = pl.BlockSpec(memory_space=pl.ANY)
    scalars = pl.BlockSpec(memory_space=pltpu.SMEM)
    operands = (
        flat(corpus_hidden),
        flat(corpus_grad),
        corpus_lengths,
        flat(query_hidden),
        flat(query_grad),
        query_lengths,
        proj_in.T,
        proj_out.T,
    )
    big = [operands[k] for k in (0, 1, 3, 4, 6, 7)]
    dma = pltpu.SemaphoreType.DMA
    steps = (proj_in.shape[0] + proj_out.shape[0]) // 1024
    scores = pl.pallas_call(
        kernel,
        out_shape=pltpu.VMEM((examples, queries * DEVICES), F32),
        in_specs=[anywhere, anywhere, scalars, anywhere, anywhere, scalars, anywhere, anywhere],
        out_specs=pl.BlockSpec(memory_space=pltpu.VMEM),
        scratch_shapes=[pltpu.VMEM(a.shape, BF16) for a in big]
        + [
            pltpu.VMEM((examples * LEN, RANK), F32),
            pltpu.VMEM((examples * LEN, RANK), F32),
            pltpu.VMEM((queries * LEN, RANK), F32),
            pltpu.VMEM((queries * LEN, RANK), F32),
            pltpu.VMEM((examples * RANK, 2 * RANK), F32),
            pltpu.VMEM((3, SIDE, SIDE, SIDE, SLAB, 2 * RANK), F32),
            pltpu.VMEM((RANK * RANK, queries * DEVICES), BF16),
            pltpu.VMEM((RANK * RANK, queries * DEVICES), BF16),
            pltpu.VMEM((RANK, 2 * RANK), F32),
            pltpu.VMEM((8, 2 * RANK), F32),
            pltpu.VMEM((MEMBERS - 1, 8, 2 * RANK), F32),
            pltpu.VMEM((CHIPS - 1, 8, 2 * RANK), F32),
            pltpu.VMEM((RANK, 2 * RANK), F32),
            pltpu.VMEM(((examples + 1) * SLAB, 2 * RANK), F32),
            pltpu.VMEM((2 * examples, RANK * RANK), BF16),
            dma((steps,)),
            dma((steps,)),
            dma((steps,)),
            dma((3,)),
            dma((3,)),
            dma((3, 7)),
            dma((3, 7)),
            dma((3,)),
            dma((3,)),
        ],
        compiler_params=pltpu.CompilerParams(
            collective_id=0, has_side_effects=True, vmem_limit_bytes=60 * 1024 * 1024
        ),
        name="influence",
    )(*operands)
    return scores


def solution(mesh):
    placed = (
        P(("corpus", "query"), None, None),
        P(("corpus", "query"), None, None),
        P(("corpus", "query")),
        P(("corpus", "query"), None, None),
        P(("corpus", "query"), None, None),
        P(("corpus", "query")),
        P(),
        P(),
    )
    return jax.shard_map(
        per_device,
        mesh=mesh,
        in_specs=placed,
        out_specs=P(("corpus", "query"), None),
        check_vma=False,
    )
```
